128 devices in a mesh: energy: 64 (over x, z, y), space: 2 (over core).
Axes of the slice: x: 4, y: 4, z: 4, core: 2. Of those that a mesh axis runs over, the one named last changes fastest.
Arguments:
- gr_diag: float32 [1024, 2, 2, 128, 128], P('energy', None, 'space'), may hold values from -1.5 to 1.5
- gr_upper: float32 [1024, 2, 2, 128, 128], P('energy', None, 'space'), may hold values from -1.5 to 1.5
- sigma_lesser: float32 [1024, 2, 2, 128, 128], P('energy', None, 'space'), may hold values from -0.18 to 0.18
- retained: int32 [2, 128, 128], P('space'), may hold values from 0 to 1, as said below
- coulomb: float32 [2, 128, 128], P('space'), may hold values from -0.5 to 0.5
Outputs:
- screened: float32 [1024, 2, 2, 128, 128], P('energy', None, 'space')
The draws below stay inside these ranges and needn't reach their ends.
Inputs may be any that keep to these rules, and one draw needn't show every extreme that they name: `retained`: entries are 0 or 1; every orbital row of every block row retains exactly 64 elements (value 1).
All inputs are finite; a program needn't handle non-finite values.
Results may differ from the reference program's by a relative error of at most 0.0003.
Values sent between devices are 32-bit elements; how exact they have to be, the bound alone decides.
A program may use at most 192 MiB of HBM per device.

```python
import math
import jax
import jax.numpy as jnp
from jax import lax

O = 128
NE = 1024
KEEP = 64
NB = 2


def draw_retained(key, part):
    scores = jax.random.randint(key, (NB, O, O), 0, 65536)
    distinct = scores * O + jnp.arange(O, dtype=jnp.int32)[None, None, :]
    ranking = jnp.argsort(jnp.argsort(distinct, axis=2), axis=2)
    return (ranking < KEEP).astype(jnp.int32)


def level_of(rng, extent, shards, smallest, high):
    def one(position, shards_of):
        draws = jax.random.uniform(jax.random.fold_in(jax.random.fold_in(rng, 6), position), (shards_of,), jnp.float32, smallest / len(shards), high / len(shards))
        return jnp.repeat(jnp.exp(draws), extent[position] // shards_of).reshape((-1,) + (1,) * (len(extent) - position - 1))

    level = one(*shards[0])
    for cut in shards[1:]:
        level = level * one(*cut)
    return level


def centred(rng, dims, scale, reach, pieces=(), kind=jnp.bfloat16):
    entries = jax.random.normal(rng, dims, jnp.float32) * scale
    if len(pieces) > 0:
        entries = level_of(rng, dims, pieces, -0.22, 0.18) * entries
    return jnp.clip(entries, min=-reach, max=reach).astype(kind)


def setup_inputs(seed: int = 0) -> dict:
    splits = jax.random.split(jax.random.key(seed), 6)
    gr_diag = centred(splits[0], (NE, 2, NB, O, O), 0.25, 1.5, ((0, 64), (2, 2)), jnp.float32)
    gr_upper = centred(splits[1], (NE, 2, NB, O, O), 0.25, 1.5, ((0, 64), (2, 2)), jnp.float32)
    sigma_lesser = centred(splits[2], (NE, 2, NB, O, O), 0.03, 0.18, ((0, 64), (2, 2)), jnp.float32)
    retained = draw_retained(jax.random.fold_in(splits[5], 71), 0)
    coulomb = centred(splits[4], (NB, O, O), O ** -0.5, 0.5, ((0, 2),), jnp.float32)
    return {"gr_diag": gr_diag, "gr_upper": gr_upper, "sigma_lesser": sigma_lesser, "retained": retained, "coulomb": coulomb}


def complex_product(left_real, left_imag, right_real, right_imag, form, conjugate):
    if conjugate:
        right_imag = -right_imag
    exact = lax.Precision.HIGHEST
    real_part = jnp.einsum(form, left_real, right_real, precision=exact) - jnp.einsum(form, left_imag, right_imag, precision=exact)
    imag_part = jnp.einsum(form, left_real, right_imag, precision=exact) + jnp.einsum(form, left_imag, right_real, precision=exact)
    return (real_part, imag_part)

def sandwich(coupling, sigma):
    partial_real, partial_imag = complex_product(coupling[:, 0], coupling[:, 1], sigma[:, 0], sigma[:, 1], 'eij,ejk->eik', False)
    result_real, result_imag = complex_product(partial_real, partial_imag, coupling[:, 0], coupling[:, 1], 'eij,ekj->eik', True)
    return jnp.stack([result_real, result_imag], axis=1)

def transposed_sandwich(coupling, sigma):
    partial_real, partial_imag = complex_product(coupling[:, 0], coupling[:, 1], sigma[:, 0], sigma[:, 1], 'eji,ejk->eik', False)
    result_real, result_imag = complex_product(partial_real, partial_imag, coupling[:, 0], coupling[:, 1], 'eij,ejk->eik', True)
    return jnp.stack([result_real, result_imag], axis=1)

def pick_row(array, row):
    return lax.dynamic_index_in_dim(array, row, 2, keepdims=False)

def reference(gr_diag, gr_upper, sigma_lesser, retained, coulomb):
    energies = gr_diag.shape[0]
    block_rows = gr_diag.shape[2]
    orbitals = gr_diag.shape[3]
    length = 2 * energies
    group = math.gcd(orbitals, 16)
    groups = orbitals // group
    mask = retained.astype(jnp.float32)
    exact = lax.Precision.HIGHEST

    def convolve(span):
        lesser_c = span[0, :, 0] + 1j * span[0, :, 1]
        greater_c = span[1, :, 0] + 1j * span[1, :, 1]
        lesser_f = jnp.fft.fft(lesser_c, n=length, axis=0)
        greater_f = jnp.fft.fft(greater_c, n=length, axis=0)
        corr = jnp.fft.ifft(lesser_f * jnp.conj(greater_f), axis=0)[:energies]
        polar = -1j * corr / math.sqrt(energies)
        return jnp.stack([jnp.real(polar), jnp.imag(polar)], axis=1)

    def one_row(index):
        below = ((index + block_rows - 1) % block_rows).astype(jnp.int32)
        above = ((index + 1) % block_rows).astype(jnp.int32)
        diagonal = pick_row(gr_diag, index)
        lesser = sandwich(diagonal, pick_row(sigma_lesser, index))
        lesser = lesser + sandwich(pick_row(gr_upper, index), pick_row(sigma_lesser, above))
        lesser = lesser + transposed_sandwich(pick_row(gr_upper, below), pick_row(sigma_lesser, below))
        spectral = jnp.stack([diagonal[:, 0] - jnp.swapaxes(diagonal[:, 0], 1, 2), diagonal[:, 1] + jnp.swapaxes(diagonal[:, 1], 1, 2)], axis=1)
        greater = lesser + spectral
        stacked = jnp.stack([lesser, greater]).reshape(2, energies, 2, groups, group, orbitals)
        stacked = jnp.moveaxis(stacked, 3, 0)
        polar = lax.map(convolve, stacked)
        polar = jnp.moveaxis(polar, 0, 2).reshape(energies, 2, orbitals, orbitals)
        polar = polar * lax.dynamic_index_in_dim(mask, index, 0, keepdims=False)[None, None]
        matrix = lax.dynamic_index_in_dim(coulomb, index, 0, keepdims=False)
        partial_value = jnp.einsum('ij,exjk->exik', matrix, polar, precision=exact)
        return jnp.einsum('exik,lk->exil', partial_value, matrix, precision=exact)
    screened = lax.map(one_row, jnp.arange(block_rows, dtype=jnp.int32))
    return jnp.moveaxis(screened, 0, 2)
```

```python
import functools
import math

import jax
import jax.numpy as jnp
import numpy as np
from jax import lax
from jax.experimental import pallas as pl
from jax.experimental.pallas import tpu as pltpu
from jax.sharding import PartitionSpec as P

MESH = pl.DeviceIdType.MESH
F32 = jnp.float32
BF16 = jnp.bfloat16

SLABS = 8
RADIX = 16
INNER = 128
CHUNKS = 2
ROWS = 8
LENGTH = RADIX * INNER


def transform_tables():
    place = np.arange(INNER)
    chunk, group, row = place // 64, (place // 8) % 8, place % 8
    n2 = 16 * group + 8 * chunk + row
    k1 = np.arange(RADIX)[:, None, None]
    k2 = np.arange(INNER)[None, :, None]
    angle = 2.0 * math.pi / LENGTH * ((n2[None, None, :] * (k1 + RADIX * k2)) % LENGTH)
    cos, sin = np.cos(angle), np.sin(angle)
    ahead = np.concatenate(
        [np.concatenate([cos, sin], axis=2), np.concatenate([-sin, cos], axis=2)], axis=1
    )
    scale = 1.0 / (LENGTH * math.sqrt(SLABS * INNER))
    back = np.swapaxes(ahead, 1, 2) * scale

    def cut(table):
        table = table.astype(np.float32)
        high = table.astype(jnp.bfloat16)
        low = (table - high.astype(np.float32)).astype(jnp.bfloat16)
        return np.stack([high, low])

    return np.stack([cut(ahead), cut(back)])


def cut(value):
    high = value.astype(BF16)
    return high, (value - high.astype(F32)).astype(BF16)


def product(left, right, transposed=False):
    dims = (((1,), (1 if transposed else 0,)), ((), ()))
    dot = functools.partial(lax.dot_general, dimension_numbers=dims, preferred_element_type=F32)
    return dot(left[0], right[0]) + dot(left[1], right[0]) + dot(left[0], right[1])


def each(fn, *pairs):
    return tuple(fn(*parts) for parts in zip(*pairs))


def beside(*parts):
    return jnp.concatenate(parts, axis=1)


def above(*parts):
    return jnp.concatenate(parts, axis=0)


def lesser_greater(gr, gi, sr, si, ur, ui, vr, vi, tr, ti):
    own_g = [cut(gr), cut(gi)]
    own_s = [cut(sr), cut(si)]
    own_u = [cut(ur), cut(ui)]
    far_u = [cut(vr), cut(vi)]
    far_s = [cut(tr), cut(ti)]
    turned_u = [cut(jnp.transpose(vr)), cut(jnp.transpose(vi))]

    def whole(pair):
        return each(lambda r, i: above(beside(r, i), beside(-i, r)), *pair)

    def conjugate(pair):
        return each(lambda r, i: above(beside(r, -i), beside(i, r)), *pair)

    first = product(each(beside, *own_g), whole(own_s))
    both = product(each(lambda a, b, c, d: above(beside(a, b), beside(c, d)), *own_u, *turned_u), whole(far_s))
    total = product(cut(first), whole(own_g), True)
    total = total + product(cut(both[:128]), whole(own_u), True)
    total = total + product(cut(both[128:]), conjugate(far_u))
    lr, li = total[:, :128], total[:, 128:]
    return lr, li, lr + (gr - jnp.transpose(gr)), li + (gi + jnp.transpose(gi))


def take(value, index):
    return jnp.take_along_axis(value, index, axis=1, mode="promise_in_bounds")


def lanes(shape):
    return lax.broadcasted_iota(jnp.int32, shape, 1)


def counts(mask):
    total = mask
    lane = lanes(mask.shape)
    for step in (1, 2, 4, 8, 16, 32, 64):
        total = total + jnp.where(lane >= step, pltpu.roll(total, step, 1), 0)
    return total


def columns_of(count):
    wanted = lanes(count.shape) % 64
    place = jnp.zeros_like(count)
    for step in (64, 32, 16, 8, 4, 2, 1):
        probe = take(count, place + (step - 1))
        place = place + jnp.where(probe <= wanted, step, 0)
    return place


def packed(value, low_index, high_index):
    low = take(value[:64], low_index)
    high = take(value[64:], high_index)
    return jnp.where(lanes(low.shape) < 64, low, high)


def unpacked(value, low_rank, high_rank, mask):
    return above(take(value, low_rank), take(value, high_rank)) * mask


def add(a, b):
    return (a[0] + b[0], a[1] + b[1])


def sub(a, b):
    return (a[0] - b[0], a[1] - b[1])


def turn(a, k, sign):
    k = k % 16
    if k >= 8:
        r, i = turn(a, k - 8, sign)
        return (-r, -i)
    if k == 0:
        return a
    if k == 4:
        return (-a[1], a[0]) if sign > 0 else (a[1], -a[0])
    c, s = math.cos(2 * math.pi * k / 16), sign * math.sin(2 * math.pi * k / 16)
    if k == 2:
        return (c * (a[0] - a[1]), c * (a[0] + a[1])) if sign > 0 else (c * (a[0] + a[1]), c * (a[1] - a[0]))
    if k == 6:
        h = -c
        return (-h * (a[0] + a[1]), h * (a[0] - a[1])) if sign > 0 else (h * (a[1] - a[0]), -h * (a[0] + a[1]))
    return (c * a[0] - s * a[1], s * a[0] + c * a[1])


def dft(values, sign):
    n = len(values)
    if n == 1:
        return values
    even, odd = dft(values[0::2], sign), dft(values[1::2], sign)
    odd = [turn(v, k * (16 // n), sign) for k, v in enumerate(odd)]
    return [add(a, b) for a, b in zip(even, odd)] + [sub(a, b) for a, b in zip(even, odd)]


def split_sixteen(values):
    even = dft(values, -1)
    odd = dft([turn(v, k, -1) for k, v in enumerate(values)], -1)
    return [v for pair in zip(even, odd) for v in pair]


def join_sixteen(values):
    even, odd = dft(values[0::2], 1), dft(values[1::2], 1)
    return [add(a, turn(b, k, 1)) for k, (a, b) in enumerate(zip(even, odd))]


def correlate(recv, table, spread, folded, psend):
    def outer(step, carry):
        chunk, group = step // 8, step % 8
        at = pl.multiple_of(step * 8, 8)
        for which in range(2):
            values = [
                (recv[chunk, n1 * 8 + group, 2 * which], recv[chunk, n1 * 8 + group, 2 * which + 1])
                for n1 in range(SLABS)
            ]
            for k1, (r, i) in enumerate(split_sixteen(values)):
                spread[k1, pl.ds(at, 8), which * 128 : (which + 1) * 128] = r
                spread[k1, pl.ds(at + 128, 8), which * 128 : (which + 1) * 128] = i
        return carry

    lax.fori_loop(0, 16, outer, 0)

    def inner(k1, carry):
        spectrum = product((table[0, 0, k1], table[0, 1, k1]), cut(spread[k1]))
        lr, li = spectrum[:128, :128], spectrum[128:, :128]
        gr, gi = spectrum[:128, 128:], spectrum[128:, 128:]
        cross = above(lr * gr + li * gi, li * gr - lr * gi)
        folded[k1] = product((table[1, 0, k1], table[1, 1, k1]), cut(cross))
        return carry

    lax.fori_loop(0, RADIX, inner, 0, unroll=2)

    def last(step, carry):
        chunk, group = step // 8, step % 8
        at = pl.multiple_of(step * 8, 8)
        values = [(folded[k1, pl.ds(at, 8)], folded[k1, pl.ds(at + 128, 8)]) for k1 in range(RADIX)]
        for n1, (r, i) in enumerate(join_sixteen(values)):
            psend[chunk, n1 * 8 + group, 0] = i
            psend[chunk, n1 * 8 + group, 1] = -r
        return carry

    lax.fori_loop(0, 16, last, 0)


def kernel(
    devices,
    g, u, s, mask, coulomb, tables, out,
    vg, vu, vs, vv, vt, table, send, recv, spread, folded, psend, precv, vout, index, rank,
    load_sem, table_sem, near_send, near_recv, send_sem, recv_sem, back_send, back_recv, out_sem,
):
    me = lax.axis_index("energy")
    side = lax.axis_index("space")
    barrier = pltpu.get_barrier_semaphore()
    pl.semaphore_signal(barrier, inc=1, device_id=(me, 1 - side), device_id_type=MESH)

    def greet(step, carry):
        pl.semaphore_signal(barrier, inc=1, device_id=(lax.rem(me + step, devices), side), device_id_type=MESH)
        return carry

    lax.fori_loop(1, devices, greet, 0)

    loads = []
    for c in range(CHUNKS):
        span = pl.ds(c * ROWS, ROWS)
        for k, (far, near) in enumerate(((g, vg), (s, vs), (u, vu))):
            loads.append(pltpu.make_async_copy(far.at[span], near.at[span], load_sem.at[c, k]))
    for copy in loads:
        copy.start()
    fetch = pltpu.make_async_copy(tables, table, table_sem)
    fetch.start()

    count = counts(mask[...])
    index[0] = columns_of(count[:64])
    index[1] = columns_of(count[64:])
    rank[0] = jnp.maximum(count[:64] - 1, 0)
    rank[1] = jnp.maximum(count[64:] + 63, 0)

    pl.semaphore_wait(barrier, devices)

    exchanges = []
    for c in range(CHUNKS):
        span = pl.ds(c * ROWS, ROWS)
        for k, (far, near) in enumerate(((s, vt), (u, vv))):
            exchanges.append(
                pltpu.make_async_remote_copy(
                    src_ref=far.at[span], dst_ref=near.at[span],
                    send_sem=near_send.at[c, k], recv_sem=near_recv.at[c, k],
                    device_id=(me, 1 - side), device_id_type=MESH,
                )
            )
    for copy in exchanges:
        copy.start()

    for c in range(CHUNKS):
        for k in range(3):
            loads[3 * c + k].wait()
        for k in range(2):
            exchanges[2 * c + k].wait_recv()

        def one_energy(row, carry):
            e = c * ROWS + row
            parts = lesser_greater(
                vg[e, 0], vg[e, 1], vs[e, 0], vs[e, 1], vu[e, 0], vu[e, 1],
                vv[e, 0], vv[e, 1], vt[e, 0], vt[e, 1],
            )
            for k, part in enumerate(parts):
                send[c, pl.ds(k * ROWS + row, devices, stride=4 * ROWS), :] = packed(part, index[0], index[1])
            return carry

        lax.fori_loop(0, ROWS, one_energy, 0)

        block = 4 * ROWS
        mine = pl.ds(pl.multiple_of(me * block, block), block)

        def give(step, carry):
            target = lax.rem(me + step, devices)
            pltpu.make_async_remote_copy(
                src_ref=send.at[c, pl.ds(pl.multiple_of(target * block, block), block)],
                dst_ref=recv.at[c, mine],
                send_sem=send_sem.at[c], recv_sem=recv_sem.at[c],
                device_id=(target, side), device_id_type=MESH,
            ).start()
            return carry

        pltpu.make_async_copy(send.at[c, mine], recv.at[c, mine], recv_sem.at[c]).start()
        lax.fori_loop(1, devices, give, 0)

    fetch.wait()
    for c in range(CHUNKS):
        pltpu.make_async_copy(recv.at[c], recv.at[c], recv_sem.at[c]).wait()

    received = recv.reshape(CHUNKS, devices, 4, ROWS, 128)
    sending = psend.reshape(CHUNKS, devices, 2, ROWS, 128)
    correlate(received, table, spread, folded, sending)

    for c in range(CHUNKS):
        block = 2 * ROWS
        mine = pl.ds(pl.multiple_of(me * block, block), block)

        def give_back(step, carry):
            target = lax.rem(me + step, devices)
            pltpu.make_async_remote_copy(
                src_ref=psend.at[c, pl.ds(pl.multiple_of(target * block, block), block)],
                dst_ref=precv.at[c, mine],
                send_sem=back_send.at[c], recv_sem=back_recv.at[c],
                device_id=(target, side), device_id_type=MESH,
            ).start()
            return carry

        pltpu.make_async_copy(psend.at[c, mine], precv.at[c, mine], back_recv.at[c]).start()
        lax.fori_loop(1, devices, give_back, 0)

    matrix = cut(coulomb[...])
    keep = mask[...].astype(F32)
    outs = []
    for c in range(CHUNKS):
        pltpu.make_async_copy(precv.at[c], precv.at[c], back_recv.at[c]).wait()

        def screen(row, carry):
            e = c * ROWS + row
            parts = [
                unpacked(
                    precv[c, pl.ds(k * ROWS + row, devices, stride=2 * ROWS), :], rank[0], rank[1], keep
                )
                for k in range(2)
            ]
            half = product(cut(above(*parts)), matrix, True)
            full = product(matrix, cut(beside(half[:128], half[128:])))
            vout[e, 0] = full[:, :128]
            vout[e, 1] = full[:, 128:]
            return carry

        lax.fori_loop(0, ROWS, screen, 0, unroll=2)
        span = pl.ds(c * ROWS, ROWS)
        outs.append(pltpu.make_async_copy(vout.at[span], out.at[span], out_sem.at[c]))
        outs[-1].start()

    for copy in exchanges:
        copy.wait_send()
    for c in range(CHUNKS):
        gone = send.at[c, pl.ds(0, (devices - 1) * 4 * ROWS)]
        pltpu.make_async_copy(gone, gone, send_sem.at[c]).wait()
        gone = psend.at[c, pl.ds(0, (devices - 1) * 2 * ROWS)]
        pltpu.make_async_copy(gone, gone, back_send.at[c]).wait()
    for copy in outs:
        copy.wait()


def on_device(devices, gr_diag, gr_upper, sigma_lesser, retained, coulomb):
    shape = gr_diag.shape
    blocks = [array.reshape(16, 2, 128, 128) for array in (gr_diag, gr_upper, sigma_lesser)]
    tables = jnp.asarray(transform_tables())
    block = pltpu.VMEM((16, 2, 128, 128), F32)
    dma = pltpu.SemaphoreType.DMA
    anywhere = pl.BlockSpec(memory_space=pl.ANY)
    near = pl.BlockSpec(memory_space=pltpu.VMEM)
    out = pl.pallas_call(
        functools.partial(kernel, devices),
        out_shape=jax.ShapeDtypeStruct((16, 2, 128, 128), F32),
        in_specs=[anywhere, anywhere, anywhere, near, near, anywhere],
        out_specs=anywhere,
        scratch_shapes=[
            block, block, block, block, block,
            pltpu.VMEM((2, 2, RADIX, 256, 256), BF16),
            pltpu.VMEM((CHUNKS, devices * 4 * ROWS, 128), F32),
            pltpu.VMEM((CHUNKS, devices * 4 * ROWS, 128), F32),
            pltpu.VMEM((RADIX, 256, 256), F32),
            pltpu.VMEM((RADIX, 256, 128), F32),
            pltpu.VMEM((CHUNKS, devices * 2 * ROWS, 128), F32),
            pltpu.VMEM((CHUNKS, devices * 2 * ROWS, 128), F32),
            block,
            pltpu.VMEM((2, 64, 128), jnp.int32),
            pltpu.VMEM((2, 64, 128), jnp.int32),
            dma((CHUNKS, 3)), dma, dma((CHUNKS, 2)), dma((CHUNKS, 2)),
            dma((CHUNKS,)), dma((CHUNKS,)), dma((CHUNKS,)), dma((CHUNKS,)), dma((CHUNKS,)),
        ],
        compiler_params=pltpu.CompilerParams(
            collective_id=0, has_side_effects=True, vmem_limit_bytes=56 * 1024 * 1024
        ),
        cost_estimate=pl.CostEstimate(flops=10**10, bytes_accessed=2 * 10**7, transcendentals=0),
    )(*blocks, retained.reshape(128, 128), coulomb.reshape(128, 128), tables)
    return out.reshape(shape)


def solution(mesh):
    whole = P("energy", None, "space", None, None)
    part = P("space", None, None)
    return jax.shard_map(
        functools.partial(on_device, mesh.shape["energy"]),
        mesh=mesh,
        in_specs=(whole, whole, whole, part, part),
        out_specs=whole,
        check_vma=False,
    )
```

```python
import functools
import math

import jax
import jax.numpy as jnp
import numpy as np
from jax import lax
from jax.experimental import pallas as pl
from jax.experimental.pallas import tpu as pltpu
from jax.sharding import PartitionSpec as P

MESH = pl.DeviceIdType.MESH
F32 = jnp.float32
BF16 = jnp.bfloat16

SLABS = 8
RADIX = 16
INNER = 128
LENGTH = RADIX * INNER
PIECES = 4
PIECE = 4
CHUNKS = 2
ROWS = 8


def high_low(table):
    table = table.astype(np.float32)
    high = table.astype(jnp.bfloat16)
    return high, (table - high.astype(np.float32)).astype(jnp.bfloat16)


def angles(n2):
    k1 = np.arange(RADIX)[:, None, None]
    k2 = np.arange(INNER)[None, :, None]
    return 2.0 * math.pi / LENGTH * ((n2[None, None, :] * (k1 + RADIX * k2)) % LENGTH)


def ahead_tables():
    tables = []
    for piece in range(PIECES):
        pair, place = np.arange(32) // 8, np.arange(32) % 8
        angle = angles(16 * (2 * pair + place // PIECE) + PIECE * piece + place % PIECE)
        cos, sin = np.cos(angle), np.sin(angle)
        real = np.concatenate([cos, sin], axis=2)
        imag = np.concatenate([-sin, cos], axis=2)
        high, low = high_low(np.concatenate([real, imag], axis=1))
        tables.append(np.concatenate([high, low, high], axis=2))
    return np.stack(tables)


def back_tables():
    scale = 1.0 / (LENGTH * math.sqrt(SLABS * INNER))
    tables = []
    for chunk in range(CHUNKS):
        group, row = np.arange(64) // 8, np.arange(64) % 8
        angle = np.swapaxes(angles(16 * group + ROWS * chunk + row), 1, 2)
        cos, sin = np.cos(angle) * scale, np.sin(angle) * scale
        real = np.concatenate([cos, -sin], axis=2)
        imag = np.concatenate([sin, cos], axis=2)
        tables.append(np.concatenate([real, imag], axis=1))
    return np.stack(high_low(np.stack(tables)))


def cut(value):
    high = value.astype(BF16)
    return high, (value - high.astype(F32)).astype(BF16)


def product(left, right, transposed=False):
    dims = (((1,), (1 if transposed else 0,)), ((), ()))
    dot = functools.partial(lax.dot_general, dimension_numbers=dims, preferred_element_type=F32)
    return dot(left[0], right[0]) + dot(left[1], right[0]) + dot(left[0], right[1])


def each(fn, *pairs):
    return tuple(fn(*parts) for parts in zip(*pairs))


def beside(*parts):
    return jnp.concatenate(parts, axis=1)


def above(*parts):
    return jnp.concatenate(parts, axis=0)


def whole(pair):
    return each(lambda r, i: above(beside(r, i), beside(-i, r)), *pair)


def conjugate(pair):
    return each(lambda r, i: above(beside(r, -i), beside(i, r)), *pair)


def lesser_greater(energies):
    held = []
    for g, s, u, v, t in energies:
        turned = [cut(jnp.transpose(part)) for part in v]
        g, s, u, v, t = ([cut(part) for part in pair] for pair in (g, s, u, v, t))
        first = product(each(beside, *g), whole(s))
        rows = each(lambda a, b, c, d: above(beside(a, b), beside(c, d)), *u, *turned)
        both = product(rows, whole(t))
        held.append((g, u, v, cut(first), cut(both[:128]), cut(both[128:])))
    results = []
    for g, u, v, first, second, third in held:
        total = product(first, whole(g), True) + product(second, whole(u), True)
        results.append(total + product(third, conjugate(v)))
    outputs = []
    for (g, *_), total in zip(energies, results):
        lr, li = total[:, :128], total[:, 128:]
        outputs.append((lr, li, lr + (g[0] - jnp.transpose(g[0])), li + (g[1] + jnp.transpose(g[1]))))
    return outputs


def take(value, index):
    return jnp.take_along_axis(value, index, axis=1, mode="promise_in_bounds")


def lanes(shape):
    return lax.broadcasted_iota(jnp.int32, shape, 1)


def counts(mask):
    total = mask
    lane = lanes(mask.shape)
    for step in (1, 2, 4, 8, 16, 32, 64):
        total = total + jnp.where(lane >= step, pltpu.roll(total, step, 1), 0)
    return total


def columns_of(count):
    wanted = lanes(count.shape) % 64
    place = jnp.zeros_like(count)
    for step in (64, 32, 16, 8, 4, 2, 1):
        probe = take(count, place + (step - 1))
        place = place + jnp.where(probe <= wanted, step, 0)
    return place


def packed(value, low_index, high_index):
    low = take(value[:64], low_index)
    high = take(value[64:], high_index)
    return jnp.where(lanes(low.shape) < 64, low, high)


def unpacked(value, low_rank, high_rank, mask):
    return above(take(value, low_rank), take(value, high_rank)) * mask


def add(a, b):
    return (a[0] + b[0], a[1] + b[1])


def sub(a, b):
    return (a[0] - b[0], a[1] - b[1])


def turn(a, k, sign):
    k = k % 16
    if k >= 8:
        r, i = turn(a, k - 8, sign)
        return (-r, -i)
    if k == 0:
        return a
    if k == 4:
        return (-a[1], a[0]) if sign > 0 else (a[1], -a[0])
    c, s = math.cos(2 * math.pi * k / 16), sign * math.sin(2 * math.pi * k / 16)
    if k == 2:
        return (c * (a[0] - a[1]), c * (a[0] + a[1])) if sign > 0 else (c * (a[0] + a[1]), c * (a[1] - a[0]))
    if k == 6:
        h = -c
        return (-h * (a[0] + a[1]), h * (a[0] - a[1])) if sign > 0 else (h * (a[1] - a[0]), -h * (a[0] + a[1]))
    return (c * a[0] - s * a[1], s * a[0] + c * a[1])


def dft(values, sign):
    n = len(values)
    if n == 1:
        return values
    even, odd = dft(values[0::2], sign), dft(values[1::2], sign)
    odd = [turn(v, k * (16 // n), sign) for k, v in enumerate(odd)]
    return [add(a, b) for a, b in zip(even, odd)] + [sub(a, b) for a, b in zip(even, odd)]


def split_sixteen(values):
    even = dft(values, -1)
    odd = dft([turn(v, k, -1) for k, v in enumerate(values)], -1)
    return [v for pair in zip(even, odd) for v in pair]


def join_sixteen(values):
    even, odd = dft(values[0::2], 1), dft(values[1::2], 1)
    return [add(a, turn(b, k, 1)) for k, (a, b) in enumerate(zip(even, odd))]


def forward(piece, recv, table, spread, spectrum):
    def outer(pair, carry):
        at = pl.multiple_of(pair * 8, 8)
        for which in range(2):
            values = []
            for n1 in range(SLABS):
                start = n1 * 8 * 16 + pair * 32 + 2 * which
                values.append(tuple(recv[piece, pl.ds(start + part, 8, stride=4), :] for part in range(2)))
            for k1, (r, i) in enumerate(split_sixteen(values)):
                spread[k1, pl.ds(at, 8), which * 128 : (which + 1) * 128] = r
                spread[k1, pl.ds(at + 32, 8), which * 128 : (which + 1) * 128] = i
        return carry

    lax.fori_loop(0, 4, outer, 0)

    def inner(step, carry):
        for k1 in [step * 4 + k for k in range(4)]:
            high, low = cut(spread[k1])
            spectrum[k1] += jnp.dot(table[piece, k1], above(high, high, low), preferred_element_type=F32)
        return carry

    lax.fori_loop(0, RADIX // 4, inner, 0)


def multiply(spectrum, cross):
    def one(k1, carry):
        lr, li = spectrum[k1, :128, :128], spectrum[k1, 128:, :128]
        gr, gi = spectrum[k1, :128, 128:], spectrum[k1, 128:, 128:]
        high, low = cut(above(lr * gr + li * gi, li * gr - lr * gi))
        cross[k1, :, :128] = high
        cross[k1, :, 128:] = low
        return carry

    lax.fori_loop(0, RADIX, one, 0, unroll=2)


def backward(chunk, table, cross, folded, psend):
    def inner(step, carry):
        for k1 in [step * 8 + k for k in range(8)]:
            both = jnp.dot(table[0, chunk, k1], cross[k1], preferred_element_type=F32)
            low = jnp.dot(table[1, chunk, k1], cross[k1, :, :128], preferred_element_type=F32)
            folded[k1] = both[:, :128] + both[:, 128:] + low
        return carry

    lax.fori_loop(0, RADIX // 8, inner, 0)

    def last(group, carry):
        at = pl.multiple_of(group * 8, 8)
        values = [(folded[k1, pl.ds(at, 8)], folded[k1, pl.ds(at + 64, 8)]) for k1 in range(RADIX)]
        for n1, (r, i) in enumerate(join_sixteen(values)):
            place = pl.multiple_of((n1 * 8 + group) * 2 * ROWS, 8)
            psend[chunk, pl.ds(place, 8), :] = i
            psend[chunk, pl.ds(place + 8, 8), :] = -r
        return carry

    lax.fori_loop(0, 8, last, 0)


def kernel(
    devices,
    g, u, s, mask, coulomb, ahead_hbm, back_hbm, out,
    vg, vu, vs, vv, vt, ahead, back, send, recv, spread, spectrum, cross, folded, psend, precv, index, rank,
    load_sem, table_sem, near_send, near_recv, send_sem, recv_sem, back_send, back_recv,
):
    me = lax.axis_index("energy")
    side = lax.axis_index("space")
    barrier = pltpu.get_barrier_semaphore()
    pl.semaphore_signal(barrier, inc=1, device_id=(me, 1 - side), device_id_type=MESH)

    def greet(step, carry):
        pl.semaphore_signal(barrier, inc=1, device_id=(lax.rem(me + step, devices), side), device_id_type=MESH)
        return carry

    lax.fori_loop(1, devices, greet, 0)

    def load(piece, k):
        span = pl.ds(piece * PIECE, PIECE)
        far, near = ((g, vg), (s, vs), (u, vu))[k]
        return pltpu.make_async_copy(far.at[span], near.at[span], load_sem.at[piece, k])

    def exchange(piece, k):
        span = pl.ds(piece * PIECE, PIECE)
        far, near = ((s, vt), (u, vv))[k]
        return pltpu.make_async_remote_copy(
            src_ref=far.at[span], dst_ref=near.at[span],
            send_sem=near_send.at[piece, k], recv_sem=near_recv.at[piece, k],
            device_id=(me, 1 - side), device_id_type=MESH,
        )

    for piece in range(PIECES):
        for k in range(3):
            load(piece, k).start()
    fetches = [
        pltpu.make_async_copy(ahead_hbm, ahead, table_sem.at[0]),
        pltpu.make_async_copy(back_hbm, back, table_sem.at[1]),
    ]

    count = counts(mask[...])
    index[0] = columns_of(count[:64])
    index[1] = columns_of(count[64:])
    rank[0] = jnp.maximum(count[:64] - 1, 0)
    rank[1] = jnp.maximum(count[64:] + 63, 0)

    pl.semaphore_wait(barrier, devices)

    for piece in range(PIECES):
        for k in range(2):
            exchange(piece, k).start()
    for copy in fetches:
        copy.start()
    spectrum[...] = jnp.zeros(spectrum.shape, F32)

    block = 4 * PIECE
    mine = pl.ds(pl.multiple_of(me * block, block), block)

    def one_piece(piece, carry):
        for k in range(3):
            load(piece, k).wait()
        for k in range(2):
            exchange(piece, k).wait_recv()
        places = [piece * PIECE + row for row in range(PIECE)]
        energies = [[(ref[e, 0], ref[e, 1]) for ref in (vg, vs, vu, vv, vt)] for e in places]
        for row, parts in enumerate(lesser_greater(energies)):
            for k, part in enumerate(parts):
                send[piece, pl.ds(row * 4 + k, devices, stride=block), :] = packed(part, index[0], index[1])

        def give(step, carry):
            target = lax.rem(me + step, devices)
            pltpu.make_async_remote_copy(
                src_ref=send.at[piece, pl.ds(pl.multiple_of(target * block, block), block)],
                dst_ref=recv.at[piece, mine],
                send_sem=send_sem.at[piece], recv_sem=recv_sem.at[piece],
                device_id=(target, side), device_id_type=MESH,
            ).start()
            return carry

        lax.fori_loop(1, devices, give, 0)
        pltpu.make_async_copy(send.at[piece, mine], recv.at[piece, mine], recv_sem.at[piece]).start()
        return carry

    lax.fori_loop(0, PIECES, one_piece, 0)

    fetches[0].wait()

    def take_in(piece, carry):
        pltpu.make_async_copy(recv.at[piece], recv.at[piece], recv_sem.at[piece]).wait()
        forward(piece, recv, ahead, spread, spectrum)
        return carry

    lax.fori_loop(0, PIECES, take_in, 0)
    multiply(spectrum, cross)
    fetches[1].wait()

    back_block = 2 * ROWS
    back_mine = pl.ds(pl.multiple_of(me * back_block, back_block), back_block)

    def return_chunk(chunk, carry):
        backward(chunk, back, cross, folded, psend)

        def give_back(step, carry):
            target = lax.rem(me + step, devices)
            pltpu.make_async_remote_copy(
                src_ref=psend.at[chunk, pl.ds(pl.multiple_of(target * back_block, back_block), back_block)],
                dst_ref=precv.at[chunk, back_mine],
                send_sem=back_send.at[chunk], recv_sem=back_recv.at[chunk],
                device_id=(target, side), device_id_type=MESH,
            ).start()
            return carry

        lax.fori_loop(1, devices, give_back, 0)
        pltpu.make_async_copy(psend.at[chunk, back_mine], precv.at[chunk, back_mine], back_recv.at[chunk]).start()
        return carry

    lax.fori_loop(0, CHUNKS, return_chunk, 0)

    matrix = cut(coulomb[...])
    twice = each(lambda m: above(beside(m, jnp.zeros_like(m)), beside(jnp.zeros_like(m), m)), matrix)
    keep = mask[...].astype(F32)

    def screen(chunk, carry):
        pltpu.make_async_copy(precv.at[chunk], precv.at[chunk], back_recv.at[chunk]).wait()
        blocks = []
        for row in range(ROWS):
            parts = [
                precv[chunk, pl.ds(k * ROWS + row, devices, stride=back_block), :] for k in range(2)
            ]
            blocks.append(beside(*[unpacked(part, rank[0], rank[1], keep) for part in parts]))
        half = product(cut(above(*blocks)), twice, True)
        high, low = cut(beside(*[half[128 * row : 128 * (row + 1)] for row in range(ROWS)]))
        full = jnp.dot(beside(*matrix), above(high, high), preferred_element_type=F32)
        full = full + jnp.dot(matrix[0], low, preferred_element_type=F32)
        for row in range(ROWS):
            out[chunk * ROWS + row, 0] = full[:, 256 * row : 256 * row + 128]
            out[chunk * ROWS + row, 1] = full[:, 256 * row + 128 : 256 * row + 256]
        return carry

    lax.fori_loop(0, CHUNKS, screen, 0)

    for piece in range(PIECES):
        for k in range(2):
            exchange(piece, k).wait_send()
        gone = send.at[piece, pl.ds(0, (devices - 1) * block)]
        pltpu.make_async_copy(gone, gone, send_sem.at[piece]).wait()
    for chunk in range(CHUNKS):
        gone = psend.at[chunk, pl.ds(0, (devices - 1) * back_block)]
        pltpu.make_async_copy(gone, gone, back_send.at[chunk]).wait()


def on_device(devices, gr_diag, gr_upper, sigma_lesser, retained, coulomb):
    shape = gr_diag.shape
    blocks = [array.reshape(16, 2, 128, 128) for array in (gr_diag, gr_upper, sigma_lesser)]
    block = pltpu.VMEM((16, 2, 128, 128), F32)
    dma = pltpu.SemaphoreType.DMA
    anywhere = pl.BlockSpec(memory_space=pl.ANY)
    near = pl.BlockSpec(memory_space=pltpu.VMEM)
    out = pl.pallas_call(
        functools.partial(kernel, devices),
        out_shape=pltpu.VMEM((16, 2, 128, 128), F32),
        in_specs=[anywhere, anywhere, anywhere, near, near, anywhere, anywhere],
        out_specs=near,
        scratch_shapes=[
            block, block, block, block, block,
            pltpu.VMEM((PIECES, RADIX, 256, 192), BF16),
            pltpu.VMEM((2, CHUNKS, RADIX, 128, 256), BF16),
            pltpu.VMEM((PIECES, devices * 4 * PIECE, 128), F32),
            pltpu.VMEM((PIECES, devices * 4 * PIECE, 128), F32),
            pltpu.VMEM((RADIX, 64, 256), F32),
            pltpu.VMEM((RADIX, 256, 256), F32),
            pltpu.VMEM((RADIX, 256, 256), BF16),
            pltpu.VMEM((RADIX, 128, 128), F32),
            pltpu.VMEM((CHUNKS, devices * 2 * ROWS, 128), F32),
            pltpu.VMEM((CHUNKS, devices * 2 * ROWS, 128), F32),
            pltpu.VMEM((2, 64, 128), jnp.int32),
            pltpu.VMEM((2, 64, 128), jnp.int32),
            dma((PIECES, 3)), dma((2,)), dma((PIECES, 2)), dma((PIECES, 2)),
            dma((PIECES,)), dma((PIECES,)), dma((CHUNKS,)), dma((CHUNKS,)),
        ],
        compiler_params=pltpu.CompilerParams(
            collective_id=0, has_side_effects=True, vmem_limit_bytes=60 * 1024 * 1024
        ),
        cost_estimate=pl.CostEstimate(flops=10**10, bytes_accessed=2 * 10**7, transcendentals=0),
    )(
        *blocks, retained.reshape(128, 128), coulomb.reshape(128, 128),
        jnp.asarray(ahead_tables()), jnp.asarray(back_tables()),
    )
    return out.reshape(shape)


def solution(mesh):
    whole = P("energy", None, "space", None, None)
    part = P("space", None, None)
    return jax.shard_map(
        functools.partial(on_device, mesh.shape["energy"]),
        mesh=mesh,
        in_specs=(whole, whole, whole, part, part),
        out_specs=whole,
        check_vma=False,
    )
```

```python
import functools
import math

import jax
import jax.numpy as jnp
import numpy as np
from jax import lax
from jax.experimental import pallas as pl
from jax.experimental.pallas import tpu as pltpu
from jax.sharding import PartitionSpec as P

MESH = pl.DeviceIdType.MESH
F32 = jnp.float32
BF16 = jnp.bfloat16

SLABS = 8
RADIX = 16
INNER = 128
LENGTH = RADIX * INNER
PIECES = 4
PIECE = 4
CHUNKS = 2
HALVES = 2
STRIDE = 11
ROWS = 8


def high_low(table):
    table = table.astype(np.float32)
    high = table.astype(jnp.bfloat16)
    return high, (table - high.astype(np.float32)).astype(jnp.bfloat16)


def angles(n2):
    k1 = np.arange(RADIX)[:, None, None]
    k2 = np.arange(INNER)[None, :, None]
    return 2.0 * math.pi / LENGTH * ((n2[None, None, :] * (k1 + RADIX * k2)) % LENGTH)


def ahead_tables():
    tables = []
    for piece in range(PIECES):
        pair, place = np.arange(32) // 8, np.arange(32) % 8
        angle = angles(16 * (2 * pair + place // PIECE) + PIECE * piece + place % PIECE)
        high, low = high_low(np.concatenate([np.cos(angle), np.sin(angle)], axis=2))
        tables.append(np.concatenate([high, low, high], axis=2))
    return np.stack(tables)


def back_tables():
    scale = 1.0 / (LENGTH * math.sqrt(SLABS * INNER))
    tables = []
    for chunk in range(CHUNKS):
        group, row = np.arange(64) // 8, np.arange(64) % 8
        angle = np.swapaxes(angles(16 * group + ROWS * chunk + row), 1, 2)
        tables.append(np.concatenate([np.cos(angle), np.sin(angle)], axis=2) * scale)
    return np.stack(high_low(np.stack(tables)))


def cut(value):
    high = value.astype(BF16)
    return high, (value - high.astype(F32)).astype(BF16)


def product(left, right, transposed=False):
    dims = (((1,), (1 if transposed else 0,)), ((), ()))
    dot = functools.partial(lax.dot_general, dimension_numbers=dims, preferred_element_type=F32)
    return dot(left[0], right[0]) + dot(left[1], right[0]) + dot(left[0], right[1])


def each(fn, *pairs):
    return tuple(fn(*parts) for parts in zip(*pairs))


def beside(*parts):
    return jnp.concatenate(parts, axis=1)


def above(*parts):
    return jnp.concatenate(parts, axis=0)


def whole(pair):
    return each(lambda r, i: above(beside(r, i), beside(-i, r)), *pair)


def conjugate(pair):
    return each(lambda r, i: above(beside(r, -i), beside(i, r)), *pair)


def own_term(energies):
    held = []
    for g, s in energies:
        g, s = ([cut(part) for part in pair] for pair in (g, s))
        held.append((g, cut(product(each(beside, *g), whole(s)))))
    return [product(first, whole(g), True) for g, first in held]


def coupled_terms(energies):
    held = []
    for u, v, t in energies:
        turned = [cut(jnp.transpose(part)) for part in v]
        u, v, t = ([cut(part) for part in pair] for pair in (u, v, t))
        rows = each(lambda a, b, c, d: above(beside(a, b), beside(c, d)), *u, *turned)
        both = product(rows, whole(t))
        held.append((u, v, cut(both[:128]), cut(both[128:])))
    return [product(second, whole(u), True) + product(third, conjugate(v)) for u, v, second, third in held]


def take(value, index):
    return jnp.take_along_axis(value, index, axis=1, mode="promise_in_bounds")


def lanes(shape):
    return lax.broadcasted_iota(jnp.int32, shape, 1)


def counts(mask):
    total = mask
    lane = lanes(mask.shape)
    for step in (1, 2, 4, 8, 16, 32, 64):
        total = total + jnp.where(lane >= step, pltpu.roll(total, step, 1), 0)
    return total


def columns_of(count):
    wanted = lanes(count.shape) % 64
    place = jnp.zeros_like(count)
    for step in (64, 32, 16, 8, 4, 2, 1):
        probe = take(count, place + (step - 1))
        place = place + jnp.where(probe <= wanted, step, 0)
    return place


def packed(lesser, greater, index):
    low, high = take(lesser, index), take(greater, index)
    return jnp.where(lanes(low.shape) < 64, low, high)


def unpacked(value, rank, mask):
    return beside(take(value, rank) * mask, take(value, rank + 64) * mask)


def add(a, b):
    return (a[0] + b[0], a[1] + b[1])


def sub(a, b):
    return (a[0] - b[0], a[1] - b[1])


def turn(a, k, sign):
    k = k % 16
    if k >= 8:
        r, i = turn(a, k - 8, sign)
        return (-r, -i)
    if k == 0:
        return a
    if k == 4:
        return (-a[1], a[0]) if sign > 0 else (a[1], -a[0])
    c, s = math.cos(2 * math.pi * k / 16), sign * math.sin(2 * math.pi * k / 16)
    if k == 2:
        return (c * (a[0] - a[1]), c * (a[0] + a[1])) if sign > 0 else (c * (a[0] + a[1]), c * (a[1] - a[0]))
    if k == 6:
        h = -c
        return (-h * (a[0] + a[1]), h * (a[0] - a[1])) if sign > 0 else (h * (a[1] - a[0]), -h * (a[0] + a[1]))
    return (c * a[0] - s * a[1], s * a[0] + c * a[1])


def dft(values, sign):
    n = len(values)
    if n == 1:
        return values
    even, odd = dft(values[0::2], sign), dft(values[1::2], sign)
    odd = [turn(v, k * (16 // n), sign) for k, v in enumerate(odd)]
    return [add(a, b) for a, b in zip(even, odd)] + [sub(a, b) for a, b in zip(even, odd)]


def split_sixteen(values):
    even = dft(values, -1)
    odd = dft([turn(v, k, -1) for k, v in enumerate(values)], -1)
    return [v for pair in zip(even, odd) for v in pair]


def join_sixteen(values):
    even, odd = dft(values[0::2], 1), dft(values[1::2], 1)
    return [add(a, turn(b, k, 1)) for k, (a, b) in enumerate(zip(even, odd))]


def forward(half, piece, recv, table, spread, spectrum):
    def outer(pair, carry):
        at = pl.multiple_of(pair * 8, 8)
        values = []
        for n1 in range(SLABS):
            start = n1 * 64 + pair * 16
            values.append(tuple(recv[half, piece, pl.ds(start + part, 8, stride=2), :] for part in range(2)))
        for k1, (r, i) in enumerate(split_sixteen(values)):
            spread[k1, pl.ds(at, 8), :] = r
            spread[k1, pl.ds(at + 32, 8), :] = i
        return carry

    lax.fori_loop(0, 4, outer, 0, unroll=2)

    def inner(step, carry):
        for k1 in [step * 8 + k for k in range(8)]:
            high, low = cut(spread[k1])
            high, low = (beside(v, above(v[32:], -v[:32])) for v in (high, low))
            spectrum[k1] += jnp.dot(table[piece, k1], above(high, high, low), preferred_element_type=F32)
        return carry

    lax.fori_loop(0, RADIX // 8, inner, 0)


def multiply(spectrum, cross):
    def one(k1, carry):
        real, imag = spectrum[k1, :, :128], spectrum[k1, :, 128:]
        real_turned, imag_turned = pltpu.roll(real, 64, 1), pltpu.roll(imag, 64, 1)
        same = real * real_turned + imag * imag_turned
        swapped = real * imag_turned - imag * real_turned
        first = lanes(same.shape) < 64
        cross[k1] = beside(*cut(above(jnp.where(first, same, swapped), jnp.where(first, swapped, same))))
        return carry

    lax.fori_loop(0, RADIX, one, 0, unroll=4)


def backward(half, chunk, table, cross, folded, psend):
    def inner(step, carry):
        for k1 in [step * 8 + k for k in range(8)]:
            both = jnp.dot(table[0, chunk, k1], cross[k1], preferred_element_type=F32)
            low = jnp.dot(table[1, chunk, k1], cross[k1, :, :128], preferred_element_type=F32)
            folded[k1] = both[:, :128] + both[:, 128:] + low
        return carry

    lax.fori_loop(0, RADIX // 8, inner, 0)

    def last(pair, carry):
        at = pl.multiple_of(pair * 16, 8)
        values = []
        for k1 in range(RADIX):
            one, two = folded[k1, pl.ds(at, 8)], folded[k1, pl.ds(at + 8, 8)]
            first = lanes(one.shape) < 64
            values.append((jnp.where(first, one, pltpu.roll(two, 64, 1)), jnp.where(first, pltpu.roll(one, 64, 1), two)))
        for n1, (r, i) in enumerate(join_sixteen(values)):
            place = pl.multiple_of((n1 * 8 + pair * 2) * ROWS, 8)
            first = lanes(r.shape) < 64
            psend[half, chunk, pl.ds(place, 8), :] = jnp.where(first, i, -pltpu.roll(r, 64, 1))
            psend[half, chunk, pl.ds(place + 8, 8), :] = jnp.where(first, pltpu.roll(i, 64, 1), -r)
        return carry

    lax.fori_loop(0, 4, last, 0)


def kernel(
    devices,
    g, u, s, mask, coulomb, ahead_hbm, back_hbm, out,
    vg, vu, vs, vv, vt, ahead, back, send, recv, spread, spectrum, cross, folded, psend, precv, half_done, index, rank, keep, own,
    load_sem, table_sem, near_send, near_recv, send_sem, recv_sem, back_send, back_recv, plane_sem, whole_sem,
):
    me = lax.axis_index("energy")
    side = lax.axis_index("space")
    barrier = pltpu.get_barrier_semaphore()
    pl.semaphore_signal(barrier, inc=1, device_id=(me, 1 - side), device_id_type=MESH)

    lines = []
    for stride in (16, 4, 1):
        digit = lax.rem(me // stride, 4)
        lines.append([me + (lax.rem(digit + step, 4) - digit) * stride for step in (1, 2, 3)])
    for line in lines:
        for other in line:
            pl.semaphore_signal(barrier, inc=1, device_id=(other, side), device_id_type=MESH)

    def load(piece, k):
        span = pl.ds(piece * PIECE, PIECE)
        far, near = ((g, vg), (s, vs), (u, vu))[k]
        return pltpu.make_async_copy(far.at[span], near.at[span], load_sem.at[piece, k])

    def exchange(piece, k):
        span = pl.ds(piece * PIECE, PIECE)
        far, near = ((s, vt), (u, vv))[k]
        return pltpu.make_async_remote_copy(
            src_ref=far.at[span], dst_ref=near.at[span],
            send_sem=near_send.at[piece, k], recv_sem=near_recv.at[piece, k],
            device_id=(me, 1 - side), device_id_type=MESH,
        )

    for piece in range(PIECES):
        for k in range(3):
            load(piece, k).start()
    fetches = [
        pltpu.make_async_copy(ahead_hbm, ahead, table_sem.at[0]),
        pltpu.make_async_copy(back_hbm, back, table_sem.at[1]),
    ]

    def local(piece):
        for k in range(2):
            load(piece, k).wait()
        places = [piece * PIECE + row for row in range(PIECE)]
        for row, term in enumerate(own_term([[(ref[e, 0], ref[e, 1]) for ref in (vg, vs)] for e in places])):
            own[row] = term

    pl.semaphore_wait(barrier, 10)

    for piece in range(PIECES):
        for k in range(2):
            exchange(piece, k).start()
    for other in lines[1]:
        pl.semaphore_signal(plane_sem, inc=1, device_id=(other, side), device_id_type=MESH)
    for copy in fetches:
        copy.start()

    count = counts(mask[...])
    for half in range(HALVES):
        rows = slice(64 * half, 64 * (half + 1))
        index[half] = columns_of(count[rows])
        rank[half] = jnp.maximum(count[rows] - 1, 0)
        keep[half] = mask[rows, :].astype(F32)

    pl.semaphore_wait(plane_sem, 3)
    for other in lines[2]:
        pl.semaphore_signal(whole_sem, inc=1, device_id=(other, side), device_id_type=MESH)
    local(0)

    mine = pl.ds(pl.multiple_of(me * 8, 8), 8)

    def spread_out(source, place, send_sems, recv_sems):
        def give(step, carry):
            target = lax.rem(me + step * STRIDE, devices)
            pltpu.make_async_remote_copy(
                src_ref=source.at[pl.ds(pl.multiple_of(target * 8, 8), 8)], dst_ref=place.at[mine],
                send_sem=send_sems, recv_sem=recv_sems, device_id=(target, side), device_id_type=MESH,
            ).start()
            return carry

        lax.fori_loop(1, devices, give, 0)
        pltpu.make_async_copy(source.at[mine], place.at[mine], recv_sems).start()

    def send_piece(half, piece):
        spread_out(send.at[half, piece], recv.at[half, piece], send_sem.at[half, piece], recv_sem.at[half, piece])

    def one_piece(piece, carry):
        load(piece, 2).wait()
        for k in range(2):
            exchange(piece, k).wait_recv()
        places = [piece * PIECE + row for row in range(PIECE)]
        terms = coupled_terms([[(ref[e, 0], ref[e, 1]) for ref in (vu, vv, vt)] for e in places])
        for row, (e, term) in enumerate(zip(places, terms)):
            term = term + own[row]
            lr, li = term[:, :128], term[:, 128:]
            gr, gi = lr + (vg[e, 0] - jnp.transpose(vg[e, 0])), li + (vg[e, 1] + jnp.transpose(vg[e, 1]))
            for half in range(HALVES):
                rows = slice(64 * half, 64 * (half + 1))
                for part, (lesser, greater) in enumerate(((lr, gr), (li, gi))):
                    send[half, piece, pl.ds(row * 2 + part, devices, stride=8), :] = packed(
                        lesser[rows], greater[rows], index[half]
                    )

        @pl.when(piece == 0)
        def _():
            pl.semaphore_wait(whole_sem, 3)

        send_piece(0, piece)

        @pl.when(piece + 1 < PIECES)
        def _():
            local(piece + 1)

        return carry

    lax.fori_loop(0, PIECES, one_piece, 0)
    for copy in fetches:
        copy.wait()

    def one_half(half, carry):
        spectrum[...] = jnp.zeros(spectrum.shape, F32)

        def take_in(piece, carry):
            @pl.when(half == 0)
            def _():
                send_piece(1, piece)

            place = recv.at[half, piece]
            pltpu.make_async_copy(place, place, recv_sem.at[half, piece]).wait()
            forward(half, piece, recv, ahead, spread, spectrum)
            return carry

        lax.fori_loop(0, PIECES, take_in, 0)
        multiply(spectrum, cross)

        def return_chunk(chunk, carry):
            backward(half, chunk, back, cross, folded, psend)
            spread_out(
                psend.at[half, chunk], precv.at[half, chunk], back_send.at[half, chunk], back_recv.at[half, chunk]
            )
            return carry

        lax.fori_loop(0, CHUNKS, return_chunk, 0)
        return carry

    lax.fori_loop(0, HALVES, one_half, 0)

    matrix = cut(coulomb[...])
    twice = each(lambda m: above(beside(m, jnp.zeros_like(m)), beside(jnp.zeros_like(m), m)), matrix)

    def narrow(half, chunk):
        place = precv.at[half, chunk]
        pltpu.make_async_copy(place, place, back_recv.at[half, chunk]).wait()
        blocks = [
            unpacked(precv[half, chunk, pl.ds(row, devices, stride=8), :], rank[half], keep[half])
            for row in range(ROWS)
        ]
        result = product(cut(above(*blocks)), twice, True)
        for row in range(ROWS):
            half_done[chunk * ROWS + row, 64 * half : 64 * (half + 1), :] = result[64 * row : 64 * (row + 1)]

    def first_half(chunk, carry):
        narrow(0, chunk)
        return carry

    lax.fori_loop(0, CHUNKS, first_half, 0)

    def finish(chunk, carry):
        narrow(1, chunk)
        high, low = cut(beside(*[half_done[chunk * ROWS + row] for row in range(ROWS)]))
        full = jnp.dot(beside(*matrix), above(high, high), preferred_element_type=F32)
        full = full + jnp.dot(matrix[0], low, preferred_element_type=F32)
        for row in range(ROWS):
            out[chunk * ROWS + row, 0] = full[:, 256 * row : 256 * row + 128]
            out[chunk * ROWS + row, 1] = full[:, 256 * row + 128 : 256 * row + 256]
        return carry

    lax.fori_loop(0, CHUNKS, finish, 0)

    for piece in range(PIECES):
        for k in range(2):
            exchange(piece, k).wait_send()
    for half in range(HALVES):
        for piece in range(PIECES):
            gone = send.at[half, piece, pl.ds(0, (devices - 1) * 8)]
            pltpu.make_async_copy(gone, gone, send_sem.at[half, piece]).wait()
        for chunk in range(CHUNKS):
            gone = psend.at[half, chunk, pl.ds(0, (devices - 1) * 8)]
            pltpu.make_async_copy(gone, gone, back_send.at[half, chunk]).wait()


def on_device(devices, gr_diag, gr_upper, sigma_lesser, retained, coulomb):
    shape = gr_diag.shape
    blocks = [array.reshape(16, 2, 128, 128) for array in (gr_diag, gr_upper, sigma_lesser)]
    block = pltpu.VMEM((16, 2, 128, 128), F32)
    dma = pltpu.SemaphoreType.DMA
    anywhere = pl.BlockSpec(memory_space=pl.ANY)
    near = pl.BlockSpec(memory_space=pltpu.VMEM)
    out = pl.pallas_call(
        functools.partial(kernel, devices),
        out_shape=pltpu.VMEM((16, 2, 128, 128), F32),
        in_specs=[anywhere, anywhere, anywhere, near, near, anywhere, anywhere],
        out_specs=near,
        scratch_shapes=[
            block, block, block, block, block,
            pltpu.VMEM((PIECES, RADIX, 128, 192), BF16),
            pltpu.VMEM((2, CHUNKS, RADIX, 64, 256), BF16),
            pltpu.VMEM((HALVES, PIECES, devices * 2 * PIECE, 128), F32),
            pltpu.VMEM((HALVES, PIECES, devices * 2 * PIECE, 128), F32),
            pltpu.VMEM((RADIX, 64, 128), F32),
            pltpu.VMEM((RADIX, 128, 256), F32),
            pltpu.VMEM((RADIX, 256, 256), BF16),
            pltpu.VMEM((RADIX, 64, 128), F32),
            pltpu.VMEM((HALVES, CHUNKS, devices * ROWS, 128), F32),
            pltpu.VMEM((HALVES, CHUNKS, devices * ROWS, 128), F32),
            pltpu.VMEM((16, 128, 256), F32),
            pltpu.VMEM((HALVES, 64, 128), jnp.int32),
            pltpu.VMEM((HALVES, 64, 128), jnp.int32),
            pltpu.VMEM((HALVES, 64, 128), F32),
            pltpu.VMEM((PIECE, 128, 256), F32),
            dma((PIECES, 3)), dma((2,)), dma((PIECES, 2)), dma((PIECES, 2)),
            dma((HALVES, PIECES)), dma((HALVES, PIECES)), dma((HALVES, CHUNKS)), dma((HALVES, CHUNKS)),
            pltpu.SemaphoreType.REGULAR, pltpu.SemaphoreType.REGULAR,
        ],
        compiler_params=pltpu.CompilerParams(
            collective_id=0, has_side_effects=True, vmem_limit_bytes=60 * 1024 * 1024
        ),
        cost_estimate=pl.CostEstimate(flops=10**10, bytes_accessed=2 * 10**7, transcendentals=0),
    )(
        *blocks, retained.reshape(128, 128), coulomb.reshape(128, 128),
        jnp.asarray(ahead_tables()), jnp.asarray(back_tables()),
    )
    return out.reshape(shape)


def solution(mesh):
    whole = P("energy", None, "space", None, None)
    part = P("space", None, None)
    return jax.shard_map(
        functools.partial(on_device, mesh.shape["energy"]),
        mesh=mesh,
        in_specs=(whole, whole, whole, part, part),
        out_specs=whole,
        check_vma=False,
    )
```

```python
import functools
import math

import jax
import jax.numpy as jnp
import numpy as np
from jax import lax
from jax.experimental import pallas as pl
from jax.experimental.pallas import tpu as pltpu
from jax.sharding import PartitionSpec as P

MESH = pl.DeviceIdType.MESH
F32 = jnp.float32
BF16 = jnp.bfloat16

SLABS = 8
RADIX = 16
INNER = 128
LENGTH = RADIX * INNER
PIECES = 4
PIECE = 4
CHUNKS = 2
HALVES = 2
BATCH = 8
STRIDE = 11
ROWS = 8


def high_low(table):
    table = table.astype(np.float32)
    high = table.astype(jnp.bfloat16)
    return high, (table - high.astype(np.float32)).astype(jnp.bfloat16)


def angles(n2):
    k1 = np.arange(RADIX)[:, None, None]
    k2 = np.arange(INNER)[None, :, None]
    return 2.0 * math.pi / LENGTH * ((n2[None, None, :] * (k1 + RADIX * k2)) % LENGTH)


def ahead_tables():
    tables = []
    for piece in range(PIECES):
        pair, place = np.arange(32) // 8, np.arange(32) % 8
        angle = angles(16 * (2 * pair + place // PIECE) + PIECE * piece + place % PIECE)
        high, low = high_low(np.concatenate([np.cos(angle), np.sin(angle)], axis=2))
        tables.append(np.concatenate([high, low, high], axis=2))
    return np.stack(tables)


def back_tables():
    scale = 1.0 / (LENGTH * math.sqrt(SLABS * INNER))
    place = np.arange(INNER)
    n2 = 16 * (place // 8 % 8) + ROWS * (place // 64) + place % 8
    angle = np.swapaxes(angles(n2), 1, 2)
    return np.stack(high_low(np.concatenate([np.cos(angle), np.sin(angle)], axis=2) * scale))


def cut(value):
    high = value.astype(BF16)
    return high, (value - high.astype(F32)).astype(BF16)


def product(left, right, transposed=False):
    dims = (((1,), (1 if transposed else 0,)), ((), ()))
    dot = functools.partial(lax.dot_general, dimension_numbers=dims, preferred_element_type=F32)
    return dot(left[0], right[0]) + dot(left[1], right[0]) + dot(left[0], right[1])


def each(fn, *pairs):
    return tuple(fn(*parts) for parts in zip(*pairs))


def beside(*parts):
    return jnp.concatenate(parts, axis=1)


def above(*parts):
    return jnp.concatenate(parts, axis=0)


def whole(pair):
    return each(lambda r, i: above(beside(r, i), beside(-i, r)), *pair)


def conjugate(pair):
    return each(lambda r, i: above(beside(r, -i), beside(i, r)), *pair)


def own_term(energies):
    held = []
    for g, s in energies:
        g, s = ([cut(part) for part in pair] for pair in (g, s))
        held.append((g, cut(product(each(beside, *g), whole(s)))))
    return [product(first, whole(g), True) for g, first in held]


def coupled_terms(energies):
    held = []
    for u, v, t in energies:
        turned = [cut(jnp.transpose(part)) for part in v]
        u, v, t = ([cut(part) for part in pair] for pair in (u, v, t))
        rows = each(lambda a, b, c, d: above(beside(a, b), beside(c, d)), *u, *turned)
        both = product(rows, whole(t))
        held.append((u, v, cut(both[:128]), cut(both[128:])))
    return [product(second, whole(u), True) + product(third, conjugate(v)) for u, v, second, third in held]


def take(value, index):
    return jnp.take_along_axis(value, index, axis=1, mode="promise_in_bounds")


def lanes(shape):
    return lax.broadcasted_iota(jnp.int32, shape, 1)


def counts(mask):
    total = mask
    lane = lanes(mask.shape)
    for step in (1, 2, 4, 8, 16, 32, 64):
        total = total + jnp.where(lane >= step, pltpu.roll(total, step, 1), 0)
    return total


def columns_of(count):
    wanted = lanes(count.shape) % 64
    place = jnp.zeros_like(count)
    for step in (64, 32, 16, 8, 4, 2, 1):
        probe = take(count, place + (step - 1))
        place = place + jnp.where(probe <= wanted, step, 0)
    return place


def packed(lesser, greater, index):
    low, high = take(lesser, index), take(greater, index)
    return jnp.where(lanes(low.shape) < 64, low, high)


def unpacked(value, rank, mask):
    return beside(take(value, rank) * mask, take(value, rank + 64) * mask)


def add(a, b):
    return (a[0] + b[0], a[1] + b[1])


def sub(a, b):
    return (a[0] - b[0], a[1] - b[1])


def turn(a, k, sign):
    k = k % 16
    if k >= 8:
        r, i = turn(a, k - 8, sign)
        return (-r, -i)
    if k == 0:
        return a
    if k == 4:
        return (-a[1], a[0]) if sign > 0 else (a[1], -a[0])
    c, s = math.cos(2 * math.pi * k / 16), sign * math.sin(2 * math.pi * k / 16)
    if k == 2:
        return (c * (a[0] - a[1]), c * (a[0] + a[1])) if sign > 0 else (c * (a[0] + a[1]), c * (a[1] - a[0]))
    if k == 6:
        h = -c
        return (-h * (a[0] + a[1]), h * (a[0] - a[1])) if sign > 0 else (h * (a[1] - a[0]), -h * (a[0] + a[1]))
    return (c * a[0] - s * a[1], s * a[0] + c * a[1])


def dft(values, sign):
    n = len(values)
    if n == 1:
        return values
    even, odd = dft(values[0::2], sign), dft(values[1::2], sign)
    odd = [turn(v, k * (16 // n), sign) for k, v in enumerate(odd)]
    return [add(a, b) for a, b in zip(even, odd)] + [sub(a, b) for a, b in zip(even, odd)]


def split_sixteen(values):
    even = dft(values, -1)
    odd = dft([turn(v, k, -1) for k, v in enumerate(values)], -1)
    return [v for pair in zip(even, odd) for v in pair]


def join_sixteen(values):
    even, odd = dft(values[0::2], 1), dft(values[1::2], 1)
    return [add(a, turn(b, k, 1)) for k, (a, b) in enumerate(zip(even, odd))]


def gather_piece(half, piece, recv, spread):
    def outer(pair, carry):
        at = pl.multiple_of(pair * 8, 8)
        values = []
        for n1 in range(SLABS):
            start = n1 * 64 + pair * 16
            values.append(tuple(recv[half, piece, pl.ds(start + part, 8, stride=2), :] for part in range(2)))
        for k1, (r, i) in enumerate(split_sixteen(values)):
            spread[k1, pl.ds(at, 8), :] = r
            spread[k1, pl.ds(at + 32, 8), :] = i
        return carry

    lax.fori_loop(0, 4, outer, 0, unroll=2)


def partial_spectrum(k1, piece, table, spread):
    high, low = cut(spread[k1])
    high, low = (beside(v, above(v[32:], -v[:32])) for v in (high, low))
    return jnp.dot(table[piece, k1], above(high, high, low), preferred_element_type=F32)


def forward(half, piece, recv, table, spread, spectrum):
    gather_piece(half, piece, recv, spread)

    def inner(step, carry):
        for k1 in [step * 8 + k for k in range(8)]:
            spectrum[k1] += partial_spectrum(k1, piece, table, spread)
        return carry

    lax.fori_loop(0, RADIX // 8, inner, 0)


def crossed(value):
    real, imag = value[:, :128], value[:, 128:]
    real_turned, imag_turned = pltpu.roll(real, 64, 1), pltpu.roll(imag, 64, 1)
    same = real * real_turned + imag * imag_turned
    swapped = real * imag_turned - imag * real_turned
    first = lanes(same.shape) < 64
    return cut(above(jnp.where(first, same, swapped), jnp.where(first, swapped, same)))


def turn_back(half, piece, recv, ahead, back, spread, spectrum, folded):
    gather_piece(half, piece, recv, spread)

    def inner(step, carry):
        places = [step * BATCH + k for k in range(BATCH)]
        pairs = [crossed(spectrum[k1] + partial_spectrum(k1, piece, ahead, spread)) for k1 in places]
        for k1, (high, low) in zip(places, pairs):
            both = jnp.dot(back[0, k1], beside(high, low), preferred_element_type=F32)
            folded[k1] = both[:, :128] + both[:, 128:] + jnp.dot(back[1, k1], high, preferred_element_type=F32)
        return carry

    lax.fori_loop(0, RADIX // BATCH, inner, 0)


def pack_back(half, chunk, folded, psend):
    def last(pair, carry):
        at = pl.multiple_of(chunk * 64 + pair * 16, 8)
        values = []
        for k1 in range(RADIX):
            one, two = folded[k1, pl.ds(at, 8)], folded[k1, pl.ds(at + 8, 8)]
            first = lanes(one.shape) < 64
            values.append((jnp.where(first, one, pltpu.roll(two, 64, 1)), jnp.where(first, pltpu.roll(one, 64, 1), two)))
        for n1, (r, i) in enumerate(join_sixteen(values)):
            place = pl.multiple_of((n1 * 8 + pair * 2) * ROWS, 8)
            first = lanes(r.shape) < 64
            psend[half, chunk, pl.ds(place, 8), :] = jnp.where(first, i, -pltpu.roll(r, 64, 1))
            psend[half, chunk, pl.ds(place + 8, 8), :] = jnp.where(first, pltpu.roll(i, 64, 1), -r)
        return carry

    lax.fori_loop(0, 4, last, 0, unroll=2)


def kernel(
    devices,
    g, u, s, mask, coulomb, ahead_hbm, back_hbm, out,
    vg, vu, vs, vv, vt, ahead, back, send, recv, spread, spectrum, folded, psend, precv, half_done, index, rank, keep, own,
    load_sem, table_sem, near_send, near_recv, send_sem, recv_sem, back_send, back_recv, plane_sem, whole_sem,
):
    me = lax.axis_index("energy")
    side = lax.axis_index("space")
    barrier = pltpu.get_barrier_semaphore()
    pl.semaphore_signal(barrier, inc=1, device_id=(me, 1 - side), device_id_type=MESH)

    lines = []
    for stride in (16, 4, 1):
        digit = lax.rem(me // stride, 4)
        lines.append([me + (lax.rem(digit + step, 4) - digit) * stride for step in (1, 2, 3)])
    for line in lines:
        for other in line:
            pl.semaphore_signal(barrier, inc=1, device_id=(other, side), device_id_type=MESH)

    def load(piece, k):
        span = pl.ds(piece * PIECE, PIECE)
        far, near = ((g, vg), (s, vs), (u, vu))[k]
        return pltpu.make_async_copy(far.at[span], near.at[span], load_sem.at[piece, k])

    def exchange(piece, k):
        span = pl.ds(piece * PIECE, PIECE)
        far, near = ((s, vt), (u, vv))[k]
        return pltpu.make_async_remote_copy(
            src_ref=far.at[span], dst_ref=near.at[span],
            send_sem=near_send.at[piece, k], recv_sem=near_recv.at[piece, k],
            device_id=(me, 1 - side), device_id_type=MESH,
        )

    for piece in range(PIECES):
        for k in range(3):
            load(piece, k).start()
    fetches = [
        pltpu.make_async_copy(ahead_hbm, ahead, table_sem.at[0]),
        pltpu.make_async_copy(back_hbm, back, table_sem.at[1]),
    ]

    def local(piece):
        for k in range(2):
            load(piece, k).wait()
        places = [piece * PIECE + row for row in range(PIECE)]
        for row, term in enumerate(own_term([[(ref[e, 0], ref[e, 1]) for ref in (vg, vs)] for e in places])):
            own[row] = term

    pl.semaphore_wait(barrier, 10)

    for piece in range(PIECES):
        for k in range(2):
            exchange(piece, k).start()
    for other in lines[1]:
        pl.semaphore_signal(plane_sem, inc=1, device_id=(other, side), device_id_type=MESH)
    for copy in fetches:
        copy.start()

    count = counts(mask[...])
    for half in range(HALVES):
        rows = slice(64 * half, 64 * (half + 1))
        index[half] = columns_of(count[rows])
        rank[half] = jnp.maximum(count[rows] - 1, 0)
        keep[half] = mask[rows, :].astype(F32)

    pl.semaphore_wait(plane_sem, 3)
    for other in lines[2]:
        pl.semaphore_signal(whole_sem, inc=1, device_id=(other, side), device_id_type=MESH)
    local(0)

    mine = pl.ds(pl.multiple_of(me * 8, 8), 8)

    def spread_out(source, place, send_to, recv_from):
        lead = (slice(None),) * (len(source.shape) - 2)

        def give(step, carry):
            target = lax.rem(me + step * STRIDE, devices)
            pltpu.make_async_remote_copy(
                src_ref=source.at[(*lead, pl.ds(pl.multiple_of(target * 8, 8), 8))], dst_ref=place.at[(*lead, mine)],
                send_sem=send_to, recv_sem=recv_from, device_id=(target, side), device_id_type=MESH,
            ).start()
            return carry

        lax.fori_loop(1, devices, give, 0, unroll=9)
        pltpu.make_async_copy(source.at[(*lead, mine)], place.at[(*lead, mine)], recv_from).start()

    def send_first(piece):
        spread_out(send.at[0, piece], recv.at[0, piece], send_sem.at[0, piece], recv_sem.at[0, piece])

    early, final = pl.ds(0, PIECES - 1), pl.ds(PIECES - 1, 1)

    def send_second(group, k):
        spread_out(send.at[1, group], recv.at[1, group], send_sem.at[1, k], recv_sem.at[1, k])

    def arrived(place, sem):
        pltpu.make_async_copy(place, place, sem).wait()

    def one_piece(piece, carry):
        load(piece, 2).wait()
        for k in range(2):
            exchange(piece, k).wait_recv()
        places = [piece * PIECE + row for row in range(PIECE)]
        terms = coupled_terms([[(ref[e, 0], ref[e, 1]) for ref in (vu, vv, vt)] for e in places])
        for row, (e, term) in enumerate(zip(places, terms)):
            term = term + own[row]
            lr, li = term[:, :128], term[:, 128:]
            gr, gi = lr + (vg[e, 0] - jnp.transpose(vg[e, 0])), li + (vg[e, 1] + jnp.transpose(vg[e, 1]))
            for half in range(HALVES):
                rows = slice(64 * half, 64 * (half + 1))
                for part, (lesser, greater) in enumerate(((lr, gr), (li, gi))):
                    send[half, piece, pl.ds(row * 2 + part, devices, stride=8), :] = packed(
                        lesser[rows], greater[rows], index[half]
                    )

        @pl.when(piece == 0)
        def _():
            pl.semaphore_wait(whole_sem, 3)

        send_first(piece)

        @pl.when(piece + 1 < PIECES)
        def _():
            local(piece + 1)

        return carry

    lax.fori_loop(0, PIECES, one_piece, 0)
    for copy in fetches:
        copy.wait()

    send_second(early, 0)
    send_second(final, 1)

    spectrum[...] = jnp.zeros(spectrum.shape, F32)

    def take_first(piece, carry):
        arrived(recv.at[0, piece], recv_sem.at[0, piece])
        forward(0, piece, recv, ahead, spread, spectrum)
        return carry

    lax.fori_loop(0, PIECES - 1, take_first, 0)
    arrived(recv.at[0, PIECES - 1], recv_sem.at[0, PIECES - 1])
    turn_back(0, PIECES - 1, recv, ahead, back, spread, spectrum, folded)
    for chunk in range(CHUNKS):
        pack_back(0, chunk, folded, psend)
    spread_out(psend.at[0], precv.at[0], back_send.at[0, 0], back_recv.at[0, 0])
    spectrum[...] = jnp.zeros(spectrum.shape, F32)
    arrived(recv.at[1, early], recv_sem.at[1, 0])

    def take_second(piece, carry):
        forward(1, piece, recv, ahead, spread, spectrum)
        return carry

    lax.fori_loop(0, PIECES - 1, take_second, 0)
    arrived(recv.at[1, final], recv_sem.at[1, 1])
    turn_back(1, PIECES - 1, recv, ahead, back, spread, spectrum, folded)

    def return_chunk(chunk, carry):
        pack_back(1, chunk, folded, psend)
        spread_out(psend.at[1, chunk], precv.at[1, chunk], back_send.at[1, chunk], back_recv.at[1, chunk])
        return carry

    lax.fori_loop(0, CHUNKS, return_chunk, 0)

    matrix = cut(coulomb[...])
    twice = each(lambda m: above(beside(m, jnp.zeros_like(m)), beside(jnp.zeros_like(m), m)), matrix)

    def narrow(half, chunk):
        blocks = [
            unpacked(precv[half, chunk, pl.ds(row, devices, stride=8), :], rank[half], keep[half])
            for row in range(ROWS)
        ]
        result = product(cut(above(*blocks)), twice, True)
        for row in range(ROWS):
            half_done[chunk * ROWS + row, 64 * half : 64 * (half + 1), :] = result[64 * row : 64 * (row + 1)]

    arrived(precv.at[0], back_recv.at[0, 0])

    def first_half(chunk, carry):
        narrow(0, chunk)
        return carry

    lax.fori_loop(0, CHUNKS, first_half, 0)

    def finish(chunk, carry):
        arrived(precv.at[1, chunk], back_recv.at[1, chunk])
        narrow(1, chunk)
        high, low = cut(beside(*[half_done[chunk * ROWS + row] for row in range(ROWS)]))
        full = jnp.dot(beside(*matrix), above(high, high), preferred_element_type=F32)
        full = full + jnp.dot(matrix[0], low, preferred_element_type=F32)
        for row in range(ROWS):
            out[chunk * ROWS + row, 0] = full[:, 256 * row : 256 * row + 128]
            out[chunk * ROWS + row, 1] = full[:, 256 * row + 128 : 256 * row + 256]
        return carry

    lax.fori_loop(0, CHUNKS, finish, 0)

    for piece in range(PIECES):
        for k in range(2):
            exchange(piece, k).wait_send()
    others = pl.ds(0, (devices - 1) * 8)
    for piece in range(PIECES):
        arrived(send.at[0, piece, others], send_sem.at[0, piece])
    arrived(send.at[1, early, others], send_sem.at[1, 0])
    arrived(send.at[1, final, others], send_sem.at[1, 1])
    arrived(psend.at[0, :, others], back_send.at[0, 0])
    for chunk in range(CHUNKS):
        arrived(psend.at[1, chunk, others], back_send.at[1, chunk])


def on_device(devices, gr_diag, gr_upper, sigma_lesser, retained, coulomb):
    shape = gr_diag.shape
    blocks = [array.reshape(16, 2, 128, 128) for array in (gr_diag, gr_upper, sigma_lesser)]
    block = pltpu.VMEM((16, 2, 128, 128), F32)
    dma = pltpu.SemaphoreType.DMA
    anywhere = pl.BlockSpec(memory_space=pl.ANY)
    near = pl.BlockSpec(memory_space=pltpu.VMEM)
    out = pl.pallas_call(
        functools.partial(kernel, devices),
        out_shape=pltpu.VMEM((16, 2, 128, 128), F32),
        in_specs=[anywhere, anywhere, anywhere, near, near, anywhere, anywhere],
        out_specs=near,
        scratch_shapes=[
            block, block, block, block, block,
            pltpu.VMEM((PIECES, RADIX, 128, 192), BF16),
            pltpu.VMEM((2, RADIX, 128, 256), BF16),
            pltpu.VMEM((HALVES, PIECES, devices * 2 * PIECE, 128), F32),
            pltpu.VMEM((HALVES, PIECES, devices * 2 * PIECE, 128), F32),
            pltpu.VMEM((RADIX, 64, 128), F32),
            pltpu.VMEM((RADIX, 128, 256), F32),
            pltpu.VMEM((RADIX, 128, 128), F32),
            pltpu.VMEM((HALVES, CHUNKS, devices * ROWS, 128), F32),
            pltpu.VMEM((HALVES, CHUNKS, devices * ROWS, 128), F32),
            pltpu.VMEM((16, 128, 256), F32),
            pltpu.VMEM((HALVES, 64, 128), jnp.int32),
            pltpu.VMEM((HALVES, 64, 128), jnp.int32),
            pltpu.VMEM((HALVES, 64, 128), F32),
            pltpu.VMEM((PIECE, 128, 256), F32),
            dma((PIECES, 3)), dma((2,)), dma((PIECES, 2)), dma((PIECES, 2)),
            dma((HALVES, PIECES)), dma((HALVES, PIECES)), dma((HALVES, CHUNKS)), dma((HALVES, CHUNKS)),
            pltpu.SemaphoreType.REGULAR, pltpu.SemaphoreType.REGULAR,
        ],
        compiler_params=pltpu.CompilerParams(
            collective_id=0, has_side_effects=True, vmem_limit_bytes=60 * 1024 * 1024
        ),
        cost_estimate=pl.CostEstimate(flops=10**10, bytes_accessed=2 * 10**7, transcendentals=0),
    )(
        *blocks, retained.reshape(128, 128), coulomb.reshape(128, 128),
        jnp.asarray(ahead_tables()), jnp.asarray(back_tables()),
    )
    return out.reshape(shape)


def solution(mesh):
    whole = P("energy", None, "space", None, None)
    part = P("space", None, None)
    return jax.shard_map(
        functools.partial(on_device, mesh.shape["energy"]),
        mesh=mesh,
        in_specs=(whole, whole, whole, part, part),
        out_specs=whole,
        check_vma=False,
    )
```

```python
import functools
import math

import jax
import jax.numpy as jnp
import numpy as np
from jax import lax
from jax.experimental import pallas as pl
from jax.experimental.pallas import tpu as pltpu
from jax.sharding import PartitionSpec as P

MESH = pl.DeviceIdType.MESH
F32 = jnp.float32
BF16 = jnp.bfloat16

SLABS = 8
RADIX = 16
INNER = 128
LENGTH = RADIX * INNER
PIECES = 4
PIECE = 4
CHUNKS = 2
HALVES = 2
BATCH = 8
STRIDE = 11
ROWS = 8


def high_low(table):
    table = table.astype(np.float32)
    high = table.astype(jnp.bfloat16)
    return high, (table - high.astype(np.float32)).astype(jnp.bfloat16)


def angles(n2):
    k1 = np.arange(RADIX)[:, None, None]
    k2 = np.arange(INNER)[None, :, None]
    return 2.0 * math.pi / LENGTH * ((n2[None, None, :] * (k1 + RADIX * k2)) % LENGTH)


def ahead_tables():
    tables = []
    for piece in range(PIECES):
        pair, place = np.arange(32) // 8, np.arange(32) % 8
        angle = angles(16 * (2 * pair + place // PIECE) + PIECE * piece + place % PIECE)
        high, low = high_low(np.concatenate([np.cos(angle), np.sin(angle)], axis=2))
        tables.append(np.concatenate([high, low, high], axis=2))
    return np.stack(tables)


def back_tables():
    scale = 1.0 / (LENGTH * math.sqrt(SLABS * INNER))
    place = np.arange(INNER)
    n2 = 16 * (place // 8 % 8) + ROWS * (place // 64) + place % 8
    angle = np.swapaxes(angles(n2), 1, 2)
    return np.stack(high_low(np.concatenate([np.cos(angle), np.sin(angle)], axis=2) * scale))


def cut(value):
    high = value.astype(BF16)
    return high, (value - high.astype(F32)).astype(BF16)


def product(left, right):
    dot = functools.partial(jnp.dot, preferred_element_type=F32)
    return dot(left[0], right[0]) + dot(left[1], right[0]) + dot(left[0], right[1])


def each(fn, *pairs):
    return tuple(fn(*parts) for parts in zip(*pairs))


def beside(*parts):
    return jnp.concatenate(parts, axis=1)


def above(*parts):
    return jnp.concatenate(parts, axis=0)


def whole(pair):
    return each(lambda r, i: above(beside(r, i), beside(-i, r)), *pair)


def conjugate(pair):
    return each(lambda r, i: above(beside(r, -i), beside(i, r)), *pair)


def own_term(energies):
    held = []
    for g, s in energies:
        turned_g = [cut(jnp.transpose(part)) for part in g]
        g, s = ([cut(part) for part in pair] for pair in (g, s))
        held.append((turned_g, cut(product(each(beside, *g), whole(s)))))
    return [product(first, conjugate(turned_g)) for turned_g, first in held]


def coupled_terms(energies):
    held = []
    for u, v, t in energies:
        turned_u, turned_v = ([cut(jnp.transpose(part)) for part in pair] for pair in (u, v))
        u, v, t = ([cut(part) for part in pair] for pair in (u, v, t))
        rows = each(lambda a, b, c, d: above(beside(a, b), beside(c, d)), *u, *turned_v)
        both = product(rows, whole(t))
        held.append((turned_u, v, cut(both[:128]), cut(both[128:])))
    return [
        product(second, conjugate(turned_u)) + product(third, conjugate(v)) for turned_u, v, second, third in held
    ]


def take(value, index):
    return jnp.take_along_axis(value, index, axis=1, mode="promise_in_bounds")


def lanes(shape):
    return lax.broadcasted_iota(jnp.int32, shape, 1)


def counts(mask):
    total = mask
    lane = lanes(mask.shape)
    for step in (1, 2, 4, 8, 16, 32, 64):
        total = total + jnp.where(lane >= step, pltpu.roll(total, step, 1), 0)
    return total


def columns_of(count):
    wanted = lanes(count.shape) % 64
    place = jnp.zeros_like(count)
    for step in (64, 32, 16, 8, 4, 2, 1):
        probe = take(count, place + (step - 1))
        place = place + jnp.where(probe <= wanted, step, 0)
    return place


def packed(lesser, greater, index):
    low, high = take(lesser, index), take(greater, index)
    return jnp.where(lanes(low.shape) < 64, low, high)


def unpacked(value, rank, mask):
    return beside(take(value, rank) * mask, take(value, rank + 64) * mask)


def add(a, b):
    return (a[0] + b[0], a[1] + b[1])


def sub(a, b):
    return (a[0] - b[0], a[1] - b[1])


def turn(a, k, sign):
    k = k % 16
    if k >= 8:
        r, i = turn(a, k - 8, sign)
        return (-r, -i)
    if k == 0:
        return a
    if k == 4:
        return (-a[1], a[0]) if sign > 0 else (a[1], -a[0])
    c, s = math.cos(2 * math.pi * k / 16), sign * math.sin(2 * math.pi * k / 16)
    if k == 2:
        return (c * (a[0] - a[1]), c * (a[0] + a[1])) if sign > 0 else (c * (a[0] + a[1]), c * (a[1] - a[0]))
    if k == 6:
        h = -c
        return (-h * (a[0] + a[1]), h * (a[0] - a[1])) if sign > 0 else (h * (a[1] - a[0]), -h * (a[0] + a[1]))
    return (c * a[0] - s * a[1], s * a[0] + c * a[1])


def dft(values, sign):
    n = len(values)
    if n == 1:
        return values
    even, odd = dft(values[0::2], sign), dft(values[1::2], sign)
    odd = [turn(v, k * (16 // n), sign) for k, v in enumerate(odd)]
    return [add(a, b) for a, b in zip(even, odd)] + [sub(a, b) for a, b in zip(even, odd)]


def split_sixteen(values):
    even = dft(values, -1)
    odd = dft([turn(v, k, -1) for k, v in enumerate(values)], -1)
    return [v for pair in zip(even, odd) for v in pair]


def join_sixteen(values):
    even, odd = dft(values[0::2], 1), dft(values[1::2], 1)
    return [add(a, turn(b, k, 1)) for k, (a, b) in enumerate(zip(even, odd))]


def gather_piece(half, piece, recv, spread):
    def outer(pair, carry):
        at = pl.multiple_of(pair * 8, 8)
        values = []
        for n1 in range(SLABS):
            start = n1 * 64 + pair * 16
            values.append(tuple(recv[half, piece, pl.ds(start + part, 8, stride=2), :] for part in range(2)))
        for k1, (r, i) in enumerate(split_sixteen(values)):
            spread[k1, pl.ds(at, 8), :] = r
            spread[k1, pl.ds(at + 32, 8), :] = i
        return carry

    lax.fori_loop(0, 4, outer, 0, unroll=2)


def partial_spectrum(k1, piece, table, spread):
    high, low = cut(spread[k1])
    high, low = (beside(v, above(v[32:], -v[:32])) for v in (high, low))
    return jnp.dot(table[piece, k1], above(high, high, low), preferred_element_type=F32)


def forward(half, piece, recv, table, spread, spectrum):
    gather_piece(half, piece, recv, spread)

    def inner(step, carry):
        for k1 in [step * 8 + k for k in range(8)]:
            spectrum[k1] += partial_spectrum(k1, piece, table, spread)
        return carry

    lax.fori_loop(0, RADIX // 8, inner, 0)


def crossed(value):
    real, imag = value[:, :128], value[:, 128:]
    real_turned, imag_turned = pltpu.roll(real, 64, 1), pltpu.roll(imag, 64, 1)
    same = real * real_turned + imag * imag_turned
    swapped = real * imag_turned - imag * real_turned
    first = lanes(same.shape) < 64
    return cut(above(jnp.where(first, same, swapped), jnp.where(first, swapped, same)))


def turn_back(half, piece, recv, ahead, back, spread, spectrum, folded):
    gather_piece(half, piece, recv, spread)

    def inner(step, carry):
        places = [step * BATCH + k for k in range(BATCH)]
        pairs = [crossed(spectrum[k1] + partial_spectrum(k1, piece, ahead, spread)) for k1 in places]
        for k1, (high, low) in zip(places, pairs):
            both = jnp.dot(back[0, k1], beside(high, low), preferred_element_type=F32)
            folded[k1] = both[:, :128] + both[:, 128:] + jnp.dot(back[1, k1], high, preferred_element_type=F32)
        return carry

    lax.fori_loop(0, RADIX // BATCH, inner, 0)


def pack_back(half, chunk, folded, psend):
    def last(pair, carry):
        at = pl.multiple_of(chunk * 64 + pair * 16, 8)
        values = []
        for k1 in range(RADIX):
            one, two = folded[k1, pl.ds(at, 8)], folded[k1, pl.ds(at + 8, 8)]
            first = lanes(one.shape) < 64
            values.append((jnp.where(first, one, pltpu.roll(two, 64, 1)), jnp.where(first, pltpu.roll(one, 64, 1), two)))
        for n1, (r, i) in enumerate(join_sixteen(values)):
            place = pl.multiple_of((n1 * 8 + pair * 2) * ROWS, 8)
            first = lanes(r.shape) < 64
            psend[half, chunk, pl.ds(place, 8), :] = jnp.where(first, i, -pltpu.roll(r, 64, 1))
            psend[half, chunk, pl.ds(place + 8, 8), :] = jnp.where(first, pltpu.roll(i, 64, 1), -r)
        return carry

    lax.fori_loop(0, 4, last, 0, unroll=2)


def kernel(
    devices,
    g, u, s, mask, coulomb, ahead_hbm, back_hbm, out,
    vg, vu, vs, vv, vt, ahead, back, send, recv, spread, spectrum, folded, psend, precv, half_done, index, rank, keep, own,
    load_sem, table_sem, near_send, near_recv, send_sem, recv_sem, back_send, back_recv, plane_sem, whole_sem,
):
    me = lax.axis_index("energy")
    side = lax.axis_index("space")
    barrier = pltpu.get_barrier_semaphore()
    pl.semaphore_signal(barrier, inc=1, device_id=(me, 1 - side), device_id_type=MESH)

    lines = []
    for stride in (16, 4, 1):
        digit = lax.rem(me // stride, 4)
        lines.append([me + (lax.rem(digit + step, 4) - digit) * stride for step in (1, 2, 3)])
    for line in lines:
        for other in line:
            pl.semaphore_signal(barrier, inc=1, device_id=(other, side), device_id_type=MESH)

    def load(piece, k):
        span = pl.ds(piece * PIECE, PIECE)
        far, near = ((g, vg), (s, vs), (u, vu))[k]
        return pltpu.make_async_copy(far.at[span], near.at[span], load_sem.at[piece, k])

    def exchange(piece, k):
        span = pl.ds(piece * PIECE, PIECE)
        far, near = ((s, vt), (u, vv))[k]
        return pltpu.make_async_remote_copy(
            src_ref=far.at[span], dst_ref=near.at[span],
            send_sem=near_send.at[piece, k], recv_sem=near_recv.at[piece, k],
            device_id=(me, 1 - side), device_id_type=MESH,
        )

    for piece in range(PIECES):
        for k in range(3):
            load(piece, k).start()
    fetches = [
        pltpu.make_async_copy(ahead_hbm, ahead, table_sem.at[0]),
        pltpu.make_async_copy(back_hbm, back, table_sem.at[1]),
    ]

    def local(piece):
        for k in range(2):
            load(piece, k).wait()
        places = [piece * PIECE + row for row in range(PIECE)]
        for row, term in enumerate(own_term([[(ref[e, 0], ref[e, 1]) for ref in (vg, vs)] for e in places])):
            own[row] = term

    pl.semaphore_wait(barrier, 10)

    for piece in range(PIECES):
        for k in range(2):
            exchange(piece, k).start()
    for other in lines[1]:
        pl.semaphore_signal(plane_sem, inc=1, device_id=(other, side), device_id_type=MESH)
    for copy in fetches:
        copy.start()

    count = counts(mask[...])
    for half in range(HALVES):
        rows = slice(64 * half, 64 * (half + 1))
        index[half] = columns_of(count[rows])
        rank[half] = jnp.maximum(count[rows] - 1, 0)
        keep[half] = mask[rows, :].astype(F32)

    pl.semaphore_wait(plane_sem, 3)
    for other in lines[2]:
        pl.semaphore_signal(whole_sem, inc=1, device_id=(other, side), device_id_type=MESH)
    local(0)

    mine = pl.ds(pl.multiple_of(me * 8, 8), 8)

    def spread_out(source, place, send_to, recv_from):
        lead = (slice(None),) * (len(source.shape) - 2)

        def give(step, carry):
            target = lax.rem(me + step * STRIDE, devices)
            pltpu.make_async_remote_copy(
                src_ref=source.at[(*lead, pl.ds(pl.multiple_of(target * 8, 8), 8))], dst_ref=place.at[(*lead, mine)],
                send_sem=send_to, recv_sem=recv_from, device_id=(target, side), device_id_type=MESH,
            ).start()
            return carry

        lax.fori_loop(1, devices, give, 0, unroll=21)
        pltpu.make_async_copy(source.at[(*lead, mine)], place.at[(*lead, mine)], recv_from).start()

    def send_first(piece):
        spread_out(send.at[0, piece], recv.at[0, piece], send_sem.at[0, piece], recv_sem.at[0, piece])

    early, final = pl.ds(0, PIECES - 1), pl.ds(PIECES - 1, 1)

    def send_second(group, k):
        spread_out(send.at[1, group], recv.at[1, group], send_sem.at[1, k], recv_sem.at[1, k])

    def arrived(place, sem):
        pltpu.make_async_copy(place, place, sem).wait()

    def one_piece(piece, carry):
        load(piece, 2).wait()
        for k in range(2):
            exchange(piece, k).wait_recv()
        places = [piece * PIECE + row for row in range(PIECE)]
        terms = coupled_terms([[(ref[e, 0], ref[e, 1]) for ref in (vu, vv, vt)] for e in places])
        for row, (e, term) in enumerate(zip(places, terms)):
            term = term + own[row]
            lr, li = term[:, :128], term[:, 128:]
            gr, gi = lr + (vg[e, 0] - jnp.transpose(vg[e, 0])), li + (vg[e, 1] + jnp.transpose(vg[e, 1]))
            for half in range(HALVES):
                rows = slice(64 * half, 64 * (half + 1))
                for part, (lesser, greater) in enumerate(((lr, gr), (li, gi))):
                    send[half, piece, pl.ds(row * 2 + part, devices, stride=8), :] = packed(
                        lesser[rows], greater[rows], index[half]
                    )

        @pl.when(piece == 0)
        def _():
            pl.semaphore_wait(whole_sem, 3)

        send_first(piece)

        @pl.when(piece + 1 < PIECES)
        def _():
            local(piece + 1)

        return carry

    lax.fori_loop(0, PIECES, one_piece, 0)
    for copy in fetches:
        copy.wait()

    send_second(early, 0)
    send_second(final, 1)

    spectrum[...] = jnp.zeros(spectrum.shape, F32)

    def take_first(piece, carry):
        arrived(recv.at[0, piece], recv_sem.at[0, piece])
        forward(0, piece, recv, ahead, spread, spectrum)
        return carry

    lax.fori_loop(0, PIECES - 1, take_first, 0)
    arrived(recv.at[0, PIECES - 1], recv_sem.at[0, PIECES - 1])
    turn_back(0, PIECES - 1, recv, ahead, back, spread, spectrum, folded)
    for chunk in range(CHUNKS):
        pack_back(0, chunk, folded, psend)
    spread_out(psend.at[0], precv.at[0], back_send.at[0, 0], back_recv.at[0, 0])
    spectrum[...] = jnp.zeros(spectrum.shape, F32)
    arrived(recv.at[1, early], recv_sem.at[1, 0])

    def take_second(piece, carry):
        forward(1, piece, recv, ahead, spread, spectrum)
        return carry

    lax.fori_loop(0, PIECES - 1, take_second, 0)
    arrived(recv.at[1, final], recv_sem.at[1, 1])
    turn_back(1, PIECES - 1, recv, ahead, back, spread, spectrum, folded)

    def return_chunk(chunk, carry):
        pack_back(1, chunk, folded, psend)
        spread_out(psend.at[1, chunk], precv.at[1, chunk], back_send.at[1, chunk], back_recv.at[1, chunk])
        return carry

    lax.fori_loop(0, CHUNKS, return_chunk, 0)

    matrix = cut(coulomb[...])
    turned_matrix = cut(jnp.transpose(coulomb[...]))
    twice = each(lambda m: above(beside(m, jnp.zeros_like(m)), beside(jnp.zeros_like(m), m)), turned_matrix)

    def narrow(half, chunk):
        blocks = [
            unpacked(precv[half, chunk, pl.ds(row, devices, stride=8), :], rank[half], keep[half])
            for row in range(ROWS)
        ]
        result = product(cut(above(*blocks)), twice)
        for row in range(ROWS):
            half_done[chunk * ROWS + row, 64 * half : 64 * (half + 1), :] = result[64 * row : 64 * (row + 1)]

    arrived(precv.at[0], back_recv.at[0, 0])

    def first_half(chunk, carry):
        narrow(0, chunk)
        return carry

    lax.fori_loop(0, CHUNKS, first_half, 0)

    def finish(chunk, carry):
        arrived(precv.at[1, chunk], back_recv.at[1, chunk])
        narrow(1, chunk)
        high, low = cut(beside(*[half_done[chunk * ROWS + row] for row in range(ROWS)]))
        full = jnp.dot(beside(*matrix), above(high, high), preferred_element_type=F32)
        full = full + jnp.dot(matrix[0], low, preferred_element_type=F32)
        for row in range(ROWS):
            out[chunk * ROWS + row, 0] = full[:, 256 * row : 256 * row + 128]
            out[chunk * ROWS + row, 1] = full[:, 256 * row + 128 : 256 * row + 256]
        return carry

    lax.fori_loop(0, CHUNKS, finish, 0)

    for piece in range(PIECES):
        for k in range(2):
            exchange(piece, k).wait_send()
    others = pl.ds(0, (devices - 1) * 8)
    for piece in range(PIECES):
        arrived(send.at[0, piece, others], send_sem.at[0, piece])
    arrived(send.at[1, early, others], send_sem.at[1, 0])
    arrived(send.at[1, final, others], send_sem.at[1, 1])
    arrived(psend.at[0, :, others], back_send.at[0, 0])
    for chunk in range(CHUNKS):
        arrived(psend.at[1, chunk, others], back_send.at[1, chunk])


def on_device(devices, gr_diag, gr_upper, sigma_lesser, retained, coulomb):
    shape = gr_diag.shape
    blocks = [array.reshape(16, 2, 128, 128) for array in (gr_diag, gr_upper, sigma_lesser)]
    block = pltpu.VMEM((16, 2, 128, 128), F32)
    dma = pltpu.SemaphoreType.DMA
    anywhere = pl.BlockSpec(memory_space=pl.ANY)
    near = pl.BlockSpec(memory_space=pltpu.VMEM)
    out = pl.pallas_call(
        functools.partial(kernel, devices),
        out_shape=pltpu.VMEM((16, 2, 128, 128), F32),
        in_specs=[anywhere, anywhere, anywhere, near, near, anywhere, anywhere],
        out_specs=near,
        scratch_shapes=[
            block, block, block, block, block,
            pltpu.VMEM((PIECES, RADIX, 128, 192), BF16),
            pltpu.VMEM((2, RADIX, 128, 256), BF16),
            pltpu.VMEM((HALVES, PIECES, devices * 2 * PIECE, 128), F32),
            pltpu.VMEM((HALVES, PIECES, devices * 2 * PIECE, 128), F32),
            pltpu.VMEM((RADIX, 64, 128), F32),
            pltpu.VMEM((RADIX, 128, 256), F32),
            pltpu.VMEM((RADIX, 128, 128), F32),
            pltpu.VMEM((HALVES, CHUNKS, devices * ROWS, 128), F32),
            pltpu.VMEM((HALVES, CHUNKS, devices * ROWS, 128), F32),
            pltpu.VMEM((16, 128, 256), F32),
            pltpu.VMEM((HALVES, 64, 128), jnp.int32),
            pltpu.VMEM((HALVES, 64, 128), jnp.int32),
            pltpu.VMEM((HALVES, 64, 128), F32),
            pltpu.VMEM((PIECE, 128, 256), F32),
            dma((PIECES, 3)), dma((2,)), dma((PIECES, 2)), dma((PIECES, 2)),
            dma((HALVES, PIECES)), dma((HALVES, PIECES)), dma((HALVES, CHUNKS)), dma((HALVES, CHUNKS)),
            pltpu.SemaphoreType.REGULAR, pltpu.SemaphoreType.REGULAR,
        ],
        compiler_params=pltpu.CompilerParams(
            collective_id=0, has_side_effects=True, vmem_limit_bytes=60 * 1024 * 1024
        ),
        cost_estimate=pl.CostEstimate(flops=10**10, bytes_accessed=2 * 10**7, transcendentals=0),
    )(
        *blocks, retained.reshape(128, 128), coulomb.reshape(128, 128),
        jnp.asarray(ahead_tables()), jnp.asarray(back_tables()),
    )
    return out.reshape(shape)


def solution(mesh):
    whole = P("energy", None, "space", None, None)
    part = P("space", None, None)
    return jax.shard_map(
        functools.partial(on_device, mesh.shape["energy"]),
        mesh=mesh,
        in_specs=(whole, whole, whole, part, part),
        out_specs=whole,
        check_vma=False,
    )
```

```python
import functools
import math

import jax
import jax.numpy as jnp
import numpy as np
from jax import lax
from jax.experimental import pallas as pl
from jax.experimental.pallas import tpu as pltpu
from jax.sharding import PartitionSpec as P

MESH = pl.DeviceIdType.MESH
F32 = jnp.float32
BF16 = jnp.bfloat16

SLABS = 8
RADIX = 16
INNER = 128
LENGTH = RADIX * INNER
PIECES = 4
PIECE = 4
CHUNKS = 2
HALVES = 2
BATCH = 8
OFFSETS = sorted(
    [(k // 16, k // 4 % 4, k % 4) for k in (step * 11 % 64 for step in range(1, 64))],
    key=lambda steps: -sum(min(step, 4 - step) for step in steps),
)
ROWS = 8


def high_low(table):
    table = table.astype(np.float32)
    high = table.astype(jnp.bfloat16)
    return high, (table - high.astype(np.float32)).astype(jnp.bfloat16)


def angles(n2):
    k1 = np.arange(RADIX)[:, None, None]
    k2 = np.arange(INNER)[None, :, None]
    return 2.0 * math.pi / LENGTH * ((n2[None, None, :] * (k1 + RADIX * k2)) % LENGTH)


def ahead_tables():
    tables = []
    for piece in range(PIECES):
        pair, place = np.arange(32) // 8, np.arange(32) % 8
        angle = angles(16 * (2 * pair + place // PIECE) + PIECE * piece + place % PIECE)
        high, low = high_low(np.concatenate([np.cos(angle), np.sin(angle)], axis=2))
        tables.append(np.concatenate([high, low, high], axis=2))
    return np.stack(tables)


def back_tables():
    scale = 1.0 / (LENGTH * math.sqrt(SLABS * INNER))
    place = np.arange(INNER)
    n2 = 16 * (place // 8 % 8) + ROWS * (place // 64) + place % 8
    angle = np.swapaxes(angles(n2), 1, 2)
    return np.stack(high_low(np.concatenate([np.cos(angle), np.sin(angle)], axis=2) * scale))


def cut(value):
    high = value.astype(BF16)
    return high, (value - high.astype(F32)).astype(BF16)


def product(left, right):
    dot = functools.partial(jnp.dot, preferred_element_type=F32)
    return dot(left[0], right[0]) + dot(left[1], right[0]) + dot(left[0], right[1])


def each(fn, *pairs):
    return tuple(fn(*parts) for parts in zip(*pairs))


def beside(*parts):
    return jnp.concatenate(parts, axis=1)


def above(*parts):
    return jnp.concatenate(parts, axis=0)


def whole(pair):
    return each(lambda r, i: above(beside(r, i), beside(-i, r)), *pair)


def conjugate(pair):
    return each(lambda r, i: above(beside(r, -i), beside(i, r)), *pair)


def own_term(energies):
    held = []
    for g, s in energies:
        turned_g = [cut(jnp.transpose(part)) for part in g]
        g, s = ([cut(part) for part in pair] for pair in (g, s))
        held.append((turned_g, cut(product(each(beside, *g), whole(s)))))
    return [product(first, conjugate(turned_g)) for turned_g, first in held]


def coupled_terms(energies):
    held = []
    for u, v, t in energies:
        turned_u, turned_v = ([cut(jnp.transpose(part)) for part in pair] for pair in (u, v))
        u, v, t = ([cut(part) for part in pair] for pair in (u, v, t))
        rows = each(lambda a, b, c, d: above(beside(a, b), beside(c, d)), *u, *turned_v)
        both = product(rows, whole(t))
        held.append((turned_u, v, cut(both[:128]), cut(both[128:])))
    return [
        product(second, conjugate(turned_u)) + product(third, conjugate(v)) for turned_u, v, second, third in held
    ]


def take(value, index):
    return jnp.take_along_axis(value, index, axis=1, mode="promise_in_bounds")


def lanes(shape):
    return lax.broadcasted_iota(jnp.int32, shape, 1)


def counts(mask):
    total = mask
    lane = lanes(mask.shape)
    for step in (1, 2, 4, 8, 16, 32, 64):
        total = total + jnp.where(lane >= step, pltpu.roll(total, step, 1), 0)
    return total


def columns_of(count):
    wanted = lanes(count.shape) % 64
    place = jnp.zeros_like(count)
    for step in (64, 32, 16, 8, 4, 2, 1):
        probe = take(count, place + (step - 1))
        place = place + jnp.where(probe <= wanted, step, 0)
    return place


def packed(lesser, greater, index):
    low, high = take(lesser, index), take(greater, index)
    return jnp.where(lanes(low.shape) < 64, low, high)


def unpacked(value, rank, mask):
    return beside(take(value, rank) * mask, take(value, rank + 64) * mask)


def add(a, b):
    return (a[0] + b[0], a[1] + b[1])


def sub(a, b):
    return (a[0] - b[0], a[1] - b[1])


def turn(a, k, sign):
    k = k % 16
    if k >= 8:
        r, i = turn(a, k - 8, sign)
        return (-r, -i)
    if k == 0:
        return a
    if k == 4:
        return (-a[1], a[0]) if sign > 0 else (a[1], -a[0])
    c, s = math.cos(2 * math.pi * k / 16), sign * math.sin(2 * math.pi * k / 16)
    if k == 2:
        return (c * (a[0] - a[1]), c * (a[0] + a[1])) if sign > 0 else (c * (a[0] + a[1]), c * (a[1] - a[0]))
    if k == 6:
        h = -c
        return (-h * (a[0] + a[1]), h * (a[0] - a[1])) if sign > 0 else (h * (a[1] - a[0]), -h * (a[0] + a[1]))
    return (c * a[0] - s * a[1], s * a[0] + c * a[1])


def dft(values, sign):
    n = len(values)
    if n == 1:
        return values
    even, odd = dft(values[0::2], sign), dft(values[1::2], sign)
    odd = [turn(v, k * (16 // n), sign) for k, v in enumerate(odd)]
    return [add(a, b) for a, b in zip(even, odd)] + [sub(a, b) for a, b in zip(even, odd)]


def split_sixteen(values):
    even = dft(values, -1)
    odd = dft([turn(v, k, -1) for k, v in enumerate(values)], -1)
    return [v for pair in zip(even, odd) for v in pair]


def join_sixteen(values):
    even, odd = dft(values[0::2], 1), dft(values[1::2], 1)
    return [add(a, turn(b, k, 1)) for k, (a, b) in enumerate(zip(even, odd))]


def gather_piece(half, piece, recv, spread):
    def outer(pair, carry):
        at = pl.multiple_of(pair * 8, 8)
        values = []
        for n1 in range(SLABS):
            start = n1 * 64 + pair * 16
            values.append(tuple(recv[half, piece, pl.ds(start + part, 8, stride=2), :] for part in range(2)))
        for k1, (r, i) in enumerate(split_sixteen(values)):
            spread[k1, pl.ds(at, 8), :] = r
            spread[k1, pl.ds(at + 32, 8), :] = i
        return carry

    lax.fori_loop(0, 4, outer, 0, unroll=2)


def partial_spectrum(k1, piece, table, spread):
    high, low = cut(spread[k1])
    high, low = (beside(v, above(v[32:], -v[:32])) for v in (high, low))
    return jnp.dot(table[piece, k1], above(high, high, low), preferred_element_type=F32)


def forward(half, piece, recv, table, spread, spectrum):
    gather_piece(half, piece, recv, spread)

    def inner(step, carry):
        for k1 in [step * 8 + k for k in range(8)]:
            spectrum[k1] += partial_spectrum(k1, piece, table, spread)
        return carry

    lax.fori_loop(0, RADIX // 8, inner, 0)


def crossed(value):
    real, imag = value[:, :128], value[:, 128:]
    real_turned, imag_turned = pltpu.roll(real, 64, 1), pltpu.roll(imag, 64, 1)
    same = real * real_turned + imag * imag_turned
    swapped = real * imag_turned - imag * real_turned
    first = lanes(same.shape) < 64
    return cut(above(jnp.where(first, same, swapped), jnp.where(first, swapped, same)))


def turn_back(half, piece, recv, ahead, back, spread, spectrum, folded):
    gather_piece(half, piece, recv, spread)

    def inner(step, carry):
        places = [step * BATCH + k for k in range(BATCH)]
        pairs = [crossed(spectrum[k1] + partial_spectrum(k1, piece, ahead, spread)) for k1 in places]
        for k1, (high, low) in zip(places, pairs):
            both = jnp.dot(back[0, k1], beside(high, low), preferred_element_type=F32)
            folded[k1] = both[:, :128] + both[:, 128:] + jnp.dot(back[1, k1], high, preferred_element_type=F32)
        return carry

    lax.fori_loop(0, RADIX // BATCH, inner, 0)


def pack_back(half, chunk, folded, psend):
    def last(pair, carry):
        at = pl.multiple_of(chunk * 64 + pair * 16, 8)
        values = []
        for k1 in range(RADIX):
            one, two = folded[k1, pl.ds(at, 8)], folded[k1, pl.ds(at + 8, 8)]
            first = lanes(one.shape) < 64
            values.append((jnp.where(first, one, pltpu.roll(two, 64, 1)), jnp.where(first, pltpu.roll(one, 64, 1), two)))
        for n1, (r, i) in enumerate(join_sixteen(values)):
            place = pl.multiple_of((n1 * 8 + pair * 2) * ROWS, 8)
            first = lanes(r.shape) < 64
            psend[half, chunk, pl.ds(place, 8), :] = jnp.where(first, i, -pltpu.roll(r, 64, 1))
            psend[half, chunk, pl.ds(place + 8, 8), :] = jnp.where(first, pltpu.roll(i, 64, 1), -r)
        return carry

    lax.fori_loop(0, 4, last, 0, unroll=2)


def kernel(
    devices,
    g, u, s, mask, coulomb, ahead_hbm, back_hbm, out,
    vg, vu, vs, vv, vt, ahead, back, send, recv, spread, spectrum, folded, psend, precv, half_done, index, rank, keep, own,
    load_sem, table_sem, near_send, near_recv, send_sem, recv_sem, back_send, back_recv, plane_sem, whole_sem,
):
    me = lax.axis_index("energy")
    side = lax.axis_index("space")
    barrier = pltpu.get_barrier_semaphore()
    pl.semaphore_signal(barrier, inc=1, device_id=(me, 1 - side), device_id_type=MESH)

    lines = []
    for stride in (16, 4, 1):
        digit = lax.rem(me // stride, 4)
        lines.append([me + (lax.rem(digit + step, 4) - digit) * stride for step in (1, 2, 3)])
    for line in lines:
        for other in line:
            pl.semaphore_signal(barrier, inc=1, device_id=(other, side), device_id_type=MESH)

    def load(piece, k):
        span = pl.ds(piece * PIECE, PIECE)
        far, near = ((g, vg), (s, vs), (u, vu))[k]
        return pltpu.make_async_copy(far.at[span], near.at[span], load_sem.at[piece, k])

    def exchange(piece, k):
        span = pl.ds(piece * PIECE, PIECE)
        far, near = ((s, vt), (u, vv))[k]
        return pltpu.make_async_remote_copy(
            src_ref=far.at[span], dst_ref=near.at[span],
            send_sem=near_send.at[piece, k], recv_sem=near_recv.at[piece, k],
            device_id=(me, 1 - side), device_id_type=MESH,
        )

    for piece in range(PIECES):
        for k in range(3):
            load(piece, k).start()
    fetches = [
        pltpu.make_async_copy(ahead_hbm, ahead, table_sem.at[0]),
        pltpu.make_async_copy(back_hbm, back, table_sem.at[1]),
    ]

    def local(piece):
        for k in range(2):
            load(piece, k).wait()
        places = [piece * PIECE + row for row in range(PIECE)]
        for row, term in enumerate(own_term([[(ref[e, 0], ref[e, 1]) for ref in (vg, vs)] for e in places])):
            own[row] = term

    pl.semaphore_wait(barrier, 10)

    for piece in range(PIECES):
        for k in range(2):
            exchange(piece, k).start()
    for other in lines[1]:
        pl.semaphore_signal(plane_sem, inc=1, device_id=(other, side), device_id_type=MESH)
    for copy in fetches:
        copy.start()

    count = counts(mask[...])
    for half in range(HALVES):
        rows = slice(64 * half, 64 * (half + 1))
        index[half] = columns_of(count[rows])
        rank[half] = jnp.maximum(count[rows] - 1, 0)
        keep[half] = mask[rows, :].astype(F32)

    pl.semaphore_wait(plane_sem, 3)
    for other in lines[2]:
        pl.semaphore_signal(whole_sem, inc=1, device_id=(other, side), device_id_type=MESH)
    local(0)

    mine = pl.ds(pl.multiple_of(me * 8, 8), 8)

    at_x, at_z, at_y = (
        [lax.rem(lax.rem(me // stride, 4) + step, 4) * stride for step in range(4)] for stride in (16, 4, 1)
    )

    def spread_out(source, place, send_to, recv_from):
        lead = (slice(None),) * (len(source.shape) - 2)

        for a, b, c in OFFSETS:
            target = at_x[a] + at_z[b] + at_y[c]
            pltpu.make_async_remote_copy(
                src_ref=source.at[(*lead, pl.ds(pl.multiple_of(target * 8, 8), 8))], dst_ref=place.at[(*lead, mine)],
                send_sem=send_to, recv_sem=recv_from, device_id=(target, side), device_id_type=MESH,
            ).start()
        pltpu.make_async_copy(source.at[(*lead, mine)], place.at[(*lead, mine)], recv_from).start()

    def send_first(piece):
        spread_out(send.at[0, piece], recv.at[0, piece], send_sem.at[0, piece], recv_sem.at[0, piece])

    early, final = pl.ds(0, PIECES - 1), pl.ds(PIECES - 1, 1)

    def send_second(group, k):
        spread_out(send.at[1, group], recv.at[1, group], send_sem.at[1, k], recv_sem.at[1, k])

    def arrived(place, sem):
        pltpu.make_async_copy(place, place, sem).wait()

    def one_piece(piece, carry):
        load(piece, 2).wait()
        for k in range(2):
            exchange(piece, k).wait_recv()
        places = [piece * PIECE + row for row in range(PIECE)]
        terms = coupled_terms([[(ref[e, 0], ref[e, 1]) for ref in (vu, vv, vt)] for e in places])
        for row, (e, term) in enumerate(zip(places, terms)):
            term = term + own[row]
            lr, li = term[:, :128], term[:, 128:]
            gr, gi = lr + (vg[e, 0] - jnp.transpose(vg[e, 0])), li + (vg[e, 1] + jnp.transpose(vg[e, 1]))
            for half in range(HALVES):
                rows = slice(64 * half, 64 * (half + 1))
                for part, (lesser, greater) in enumerate(((lr, gr), (li, gi))):
                    send[half, piece, pl.ds(row * 2 + part, devices, stride=8), :] = packed(
                        lesser[rows], greater[rows], index[half]
                    )

        @pl.when(piece == 0)
        def _():
            pl.semaphore_wait(whole_sem, 3)

        send_first(piece)

        @pl.when(piece + 1 < PIECES)
        def _():
            local(piece + 1)

        return carry

    lax.fori_loop(0, PIECES, one_piece, 0)
    for copy in fetches:
        copy.wait()

    send_second(early, 0)
    send_second(final, 1)

    spectrum[...] = jnp.zeros(spectrum.shape, F32)

    def take_first(piece, carry):
        arrived(recv.at[0, piece], recv_sem.at[0, piece])
        forward(0, piece, recv, ahead, spread, spectrum)
        return carry

    lax.fori_loop(0, PIECES - 1, take_first, 0)
    arrived(recv.at[0, PIECES - 1], recv_sem.at[0, PIECES - 1])
    turn_back(0, PIECES - 1, recv, ahead, back, spread, spectrum, folded)
    for chunk in range(CHUNKS):
        pack_back(0, chunk, folded, psend)
    spread_out(psend.at[0], precv.at[0], back_send.at[0, 0], back_recv.at[0, 0])
    spectrum[...] = jnp.zeros(spectrum.shape, F32)
    arrived(recv.at[1, early], recv_sem.at[1, 0])

    def take_second(piece, carry):
        forward(1, piece, recv, ahead, spread, spectrum)
        return carry

    lax.fori_loop(0, PIECES - 1, take_second, 0)
    arrived(recv.at[1, final], recv_sem.at[1, 1])
    turn_back(1, PIECES - 1, recv, ahead, back, spread, spectrum, folded)

    def return_chunk(chunk, carry):
        pack_back(1, chunk, folded, psend)
        spread_out(psend.at[1, chunk], precv.at[1, chunk], back_send.at[1, chunk], back_recv.at[1, chunk])
        return carry

    lax.fori_loop(0, CHUNKS, return_chunk, 0)

    matrix = cut(coulomb[...])
    turned_matrix = cut(jnp.transpose(coulomb[...]))
    twice = each(lambda m: above(beside(m, jnp.zeros_like(m)), beside(jnp.zeros_like(m), m)), turned_matrix)

    def narrow(half, chunk):
        blocks = [
            unpacked(precv[half, chunk, pl.ds(row, devices, stride=8), :], rank[half], keep[half])
            for row in range(ROWS)
        ]
        result = product(cut(above(*blocks)), twice)
        for row in range(ROWS):
            half_done[chunk * ROWS + row, 64 * half : 64 * (half + 1), :] = result[64 * row : 64 * (row + 1)]

    arrived(precv.at[0], back_recv.at[0, 0])

    def first_half(chunk, carry):
        narrow(0, chunk)
        return carry

    lax.fori_loop(0, CHUNKS, first_half, 0)

    def finish(chunk, carry):
        arrived(precv.at[1, chunk], back_recv.at[1, chunk])
        narrow(1, chunk)
        high, low = cut(beside(*[half_done[chunk * ROWS + row] for row in range(ROWS)]))
        full = jnp.dot(beside(*matrix), above(high, high), preferred_element_type=F32)
        full = full + jnp.dot(matrix[0], low, preferred_element_type=F32)
        for row in range(ROWS):
            out[chunk * ROWS + row, 0] = full[:, 256 * row : 256 * row + 128]
            out[chunk * ROWS + row, 1] = full[:, 256 * row + 128 : 256 * row + 256]
        return carry

    lax.fori_loop(0, CHUNKS, finish, 0)

    for piece in range(PIECES):
        for k in range(2):
            exchange(piece, k).wait_send()
    others = pl.ds(0, (devices - 1) * 8)
    for piece in range(PIECES):
        arrived(send.at[0, piece, others], send_sem.at[0, piece])
    arrived(send.at[1, early, others], send_sem.at[1, 0])
    arrived(send.at[1, final, others], send_sem.at[1, 1])
    arrived(psend.at[0, :, others], back_send.at[0, 0])
    for chunk in range(CHUNKS):
        arrived(psend.at[1, chunk, others], back_send.at[1, chunk])


def on_device(devices, gr_diag, gr_upper, sigma_lesser, retained, coulomb):
    shape = gr_diag.shape
    blocks = [array.reshape(16, 2, 128, 128) for array in (gr_diag, gr_upper, sigma_lesser)]
    block = pltpu.VMEM((16, 2, 128, 128), F32)
    dma = pltpu.SemaphoreType.DMA
    anywhere = pl.BlockSpec(memory_space=pl.ANY)
    near = pl.BlockSpec(memory_space=pltpu.VMEM)
    out = pl.pallas_call(
        functools.partial(kernel, devices),
        out_shape=pltpu.VMEM((16, 2, 128, 128), F32),
        in_specs=[anywhere, anywhere, anywhere, near, near, anywhere, anywhere],
        out_specs=near,
        scratch_shapes=[
            block, block, block, block, block,
            pltpu.VMEM((PIECES, RADIX, 128, 192), BF16),
            pltpu.VMEM((2, RADIX, 128, 256), BF16),
            pltpu.VMEM((HALVES, PIECES, devices * 2 * PIECE, 128), F32),
            pltpu.VMEM((HALVES, PIECES, devices * 2 * PIECE, 128), F32),
            pltpu.VMEM((RADIX, 64, 128), F32),
            pltpu.VMEM((RADIX, 128, 256), F32),
            pltpu.VMEM((RADIX, 128, 128), F32),
            pltpu.VMEM((HALVES, CHUNKS, devices * ROWS, 128), F32),
            pltpu.VMEM((HALVES, CHUNKS, devices * ROWS, 128), F32),
            pltpu.VMEM((16, 128, 256), F32),
            pltpu.VMEM((HALVES, 64, 128), jnp.int32),
            pltpu.VMEM((HALVES, 64, 128), jnp.int32),
            pltpu.VMEM((HALVES, 64, 128), F32),
            pltpu.VMEM((PIECE, 128, 256), F32),
            dma((PIECES, 3)), dma((2,)), dma((PIECES, 2)), dma((PIECES, 2)),
            dma((HALVES, PIECES)), dma((HALVES, PIECES)), dma((HALVES, CHUNKS)), dma((HALVES, CHUNKS)),
            pltpu.SemaphoreType.REGULAR, pltpu.SemaphoreType.REGULAR,
        ],
        compiler_params=pltpu.CompilerParams(
            collective_id=0, has_side_effects=True, vmem_limit_bytes=60 * 1024 * 1024
        ),
        cost_estimate=pl.CostEstimate(flops=10**10, bytes_accessed=2 * 10**7, transcendentals=0),
    )(
        *blocks, retained.reshape(128, 128), coulomb.reshape(128, 128),
        jnp.asarray(ahead_tables()), jnp.asarray(back_tables()),
    )
    return out.reshape(shape)


def solution(mesh):
    whole = P("energy", None, "space", None, None)
    part = P("space", None, None)
    return jax.shard_map(
        functools.partial(on_device, mesh.shape["energy"]),
        mesh=mesh,
        in_specs=(whole, whole, whole, part, part),
        out_specs=whole,
        check_vma=False,
    )
```

```python
import functools
import math

import jax
import jax.numpy as jnp
import numpy as np
from jax import lax
from jax.experimental import pallas as pl
from jax.experimental.pallas import tpu as pltpu
from jax.sharding import PartitionSpec as P

MESH = pl.DeviceIdType.MESH
F32 = jnp.float32
BF16 = jnp.bfloat16

SLABS = 8
RADIX = 16
INNER = 128
LENGTH = RADIX * INNER
PIECES = 4
PIECE = 4
CHUNKS = 2
HALVES = 2
BATCH = 8
OFFSETS = sorted(
    [(k // 16, k // 4 % 4, k % 4) for k in (step * 11 % 64 for step in range(1, 64))],
    key=lambda steps: -sum(min(step, 4 - step) for step in steps),
)
ROWS = 8


def high_low(table):
    table = table.astype(np.float32)
    high = table.astype(jnp.bfloat16)
    return high, (table - high.astype(np.float32)).astype(jnp.bfloat16)


def angles(n2):
    k1 = np.arange(RADIX)[:, None, None]
    k2 = np.arange(INNER)[None, :, None]
    return 2.0 * math.pi / LENGTH * ((n2[None, None, :] * (k1 + RADIX * k2)) % LENGTH)


def ahead_tables():
    tables = []
    for piece in range(PIECES):
        pair, place = np.arange(32) // 8, np.arange(32) % 8
        angle = angles(16 * (2 * pair + place // PIECE) + PIECE * piece + place % PIECE)
        high, low = high_low(np.concatenate([np.cos(angle), np.sin(angle)], axis=2))
        tables.append(np.concatenate([high, low, high], axis=2))
    return np.stack(tables)


def back_tables():
    scale = 1.0 / (LENGTH * math.sqrt(SLABS * INNER))
    place = np.arange(INNER)
    n2 = 16 * (place // 8 % 8) + ROWS * (place // 64) + place % 8
    angle = np.swapaxes(angles(n2), 1, 2)
    return np.stack(high_low(np.concatenate([np.cos(angle), np.sin(angle)], axis=2) * scale))


def cut(value):
    high = value.astype(BF16)
    return high, (value - high.astype(F32)).astype(BF16)


def product(left, right):
    dot = functools.partial(jnp.dot, preferred_element_type=F32)
    return dot(left[0], right[0]) + dot(left[1], right[0]) + dot(left[0], right[1])


def each(fn, *pairs):
    return tuple(fn(*parts) for parts in zip(*pairs))


def beside(*parts):
    return jnp.concatenate(parts, axis=1)


def above(*parts):
    return jnp.concatenate(parts, axis=0)


def whole(pair):
    return each(lambda r, i: above(beside(r, i), beside(-i, r)), *pair)


def conjugate(pair):
    return each(lambda r, i: above(beside(r, -i), beside(i, r)), *pair)


def own_term(energies):
    held = []
    for g, s in energies:
        turned_g = [cut(jnp.transpose(part)) for part in g]
        g, s = ([cut(part) for part in pair] for pair in (g, s))
        held.append((turned_g, cut(product(each(beside, *g), whole(s)))))
    return [product(first, conjugate(turned_g)) for turned_g, first in held]


def coupled_terms(energies):
    held = []
    for u, v, t in energies:
        turned_u, turned_v = ([cut(jnp.transpose(part)) for part in pair] for pair in (u, v))
        u, v, t = ([cut(part) for part in pair] for pair in (u, v, t))
        rows = each(lambda a, b, c, d: above(beside(a, b), beside(c, d)), *u, *turned_v)
        both = product(rows, whole(t))
        held.append((turned_u, v, cut(both[:128]), cut(both[128:])))
    return [
        product(second, conjugate(turned_u)) + product(third, conjugate(v)) for turned_u, v, second, third in held
    ]


def take(value, index):
    return jnp.take_along_axis(value, index, axis=1, mode="promise_in_bounds")


def lanes(shape):
    return lax.broadcasted_iota(jnp.int32, shape, 1)


def counts(mask):
    total = mask
    lane = lanes(mask.shape)
    for step in (1, 2, 4, 8, 16, 32, 64):
        total = total + jnp.where(lane >= step, pltpu.roll(total, step, 1), 0)
    return total


def columns_of(count):
    wanted = lanes(count.shape) % 64
    place = jnp.zeros_like(count)
    for step in (64, 32, 16, 8, 4, 2, 1):
        probe = take(count, place + (step - 1))
        place = place + jnp.where(probe <= wanted, step, 0)
    return place


def packed(lesser, greater, index):
    low, high = take(lesser, index), take(greater, index)
    return jnp.where(lanes(low.shape) < 64, low, high)


def unpacked(value, rank, mask):
    return beside(take(value, rank) * mask, take(value, rank + 64) * mask)


def add(a, b):
    return (a[0] + b[0], a[1] + b[1])


def sub(a, b):
    return (a[0] - b[0], a[1] - b[1])


def turn(a, k, sign):
    k = k % 16
    if k >= 8:
        r, i = turn(a, k - 8, sign)
        return (-r, -i)
    if k == 0:
        return a
    if k == 4:
        return (-a[1], a[0]) if sign > 0 else (a[1], -a[0])
    c, s = math.cos(2 * math.pi * k / 16), sign * math.sin(2 * math.pi * k / 16)
    if k == 2:
        return (c * (a[0] - a[1]), c * (a[0] + a[1])) if sign > 0 else (c * (a[0] + a[1]), c * (a[1] - a[0]))
    if k == 6:
        h = -c
        return (-h * (a[0] + a[1]), h * (a[0] - a[1])) if sign > 0 else (h * (a[1] - a[0]), -h * (a[0] + a[1]))
    return (c * a[0] - s * a[1], s * a[0] + c * a[1])


def dft(values, sign):
    n = len(values)
    if n == 1:
        return values
    even, odd = dft(values[0::2], sign), dft(values[1::2], sign)
    odd = [turn(v, k * (16 // n), sign) for k, v in enumerate(odd)]
    return [add(a, b) for a, b in zip(even, odd)] + [sub(a, b) for a, b in zip(even, odd)]


def split_sixteen(values):
    even = dft(values, -1)
    odd = dft([turn(v, k, -1) for k, v in enumerate(values)], -1)
    return [v for pair in zip(even, odd) for v in pair]


def join_sixteen(values):
    even, odd = dft(values[0::2], 1), dft(values[1::2], 1)
    return [add(a, turn(b, k, 1)) for k, (a, b) in enumerate(zip(even, odd))]


def gather_piece(half, piece, recv, spread):
    def outer(pair, carry):
        at = pl.multiple_of(pair * 8, 8)
        values = []
        for n1 in range(SLABS):
            start = n1 * 64 + pair * 16
            values.append(tuple(recv[half, piece, pl.ds(start + part, 8, stride=2), :] for part in range(2)))
        for k1, (r, i) in enumerate(split_sixteen(values)):
            spread[k1, pl.ds(at, 8), :] = r
            spread[k1, pl.ds(at + 32, 8), :] = i
        return carry

    lax.fori_loop(0, 4, outer, 0, unroll=2)


def partial_spectrum(k1, piece, table, spread):
    high, low = cut(spread[k1])
    high, low = (beside(v, above(v[32:], -v[:32])) for v in (high, low))
    return jnp.dot(table[piece, k1], above(high, high, low), preferred_element_type=F32)


def forward(half, piece, recv, table, spread, spectrum):
    gather_piece(half, piece, recv, spread)

    def inner(step, carry):
        for k1 in [step * 8 + k for k in range(8)]:
            spectrum[k1] += partial_spectrum(k1, piece, table, spread)
        return carry

    lax.fori_loop(0, RADIX // 8, inner, 0)


def crossed(value):
    real, imag = value[:, :128], value[:, 128:]
    real_turned, imag_turned = pltpu.roll(real, 64, 1), pltpu.roll(imag, 64, 1)
    same = real * real_turned + imag * imag_turned
    swapped = real * imag_turned - imag * real_turned
    first = lanes(same.shape) < 64
    return cut(above(jnp.where(first, same, swapped), jnp.where(first, swapped, same)))


def turn_back(half, piece, recv, ahead, back, spread, spectrum, folded):
    gather_piece(half, piece, recv, spread)

    def inner(step, carry):
        places = [step * BATCH + k for k in range(BATCH)]
        pairs = [crossed(spectrum[k1] + partial_spectrum(k1, piece, ahead, spread)) for k1 in places]
        for k1, (high, low) in zip(places, pairs):
            both = jnp.dot(back[0, k1], beside(high, low), preferred_element_type=F32)
            folded[k1] = both[:, :128] + both[:, 128:] + jnp.dot(back[1, k1], high, preferred_element_type=F32)
        return carry

    lax.fori_loop(0, RADIX // BATCH, inner, 0)


def pack_back(half, chunk, folded, psend):
    def last(pair, carry):
        at = pl.multiple_of(chunk * 64 + pair * 16, 8)
        values = []
        for k1 in range(RADIX):
            one, two = folded[k1, pl.ds(at, 8)], folded[k1, pl.ds(at + 8, 8)]
            first = lanes(one.shape) < 64
            values.append((jnp.where(first, one, pltpu.roll(two, 64, 1)), jnp.where(first, pltpu.roll(one, 64, 1), two)))
        for n1, (r, i) in enumerate(join_sixteen(values)):
            place = pl.multiple_of((n1 * 8 + pair * 2) * ROWS, 8)
            first = lanes(r.shape) < 64
            psend[half, chunk, pl.ds(place, 8), :] = jnp.where(first, i, -pltpu.roll(r, 64, 1))
            psend[half, chunk, pl.ds(place + 8, 8), :] = jnp.where(first, pltpu.roll(i, 64, 1), -r)
        return carry

    lax.fori_loop(0, 4, last, 0, unroll=2)


def kernel(
    devices,
    g, u, s, mask, coulomb, ahead_hbm, back_hbm, out,
    vg, vu, vs, vv, vt, ahead, back, send, recv, spread, spectrum, folded, psend, precv, half_done, index, rank, keep, own,
    load_sem, table_sem, near_send, near_recv, send_sem, recv_sem, back_send, back_recv, plane_sem, whole_sem,
):
    me = lax.axis_index("energy")
    side = lax.axis_index("space")
    barrier = pltpu.get_barrier_semaphore()
    pl.semaphore_signal(barrier, inc=1, device_id=(me, 1 - side), device_id_type=MESH)

    lines = []
    for stride in (16, 4, 1):
        digit = lax.rem(me // stride, 4)
        lines.append([me + (lax.rem(digit + step, 4) - digit) * stride for step in (1, 2, 3)])
    for line in lines:
        for other in line:
            pl.semaphore_signal(barrier, inc=1, device_id=(other, side), device_id_type=MESH)

    def load(piece, k):
        span = pl.ds(piece * PIECE, PIECE)
        far, near = ((g, vg), (s, vs), (u, vu))[k]
        return pltpu.make_async_copy(far.at[span], near.at[span], load_sem.at[piece, k])

    def exchange(piece, k):
        span = pl.ds(piece * PIECE, PIECE)
        far, near = ((s, vt), (u, vv))[k]
        return pltpu.make_async_remote_copy(
            src_ref=far.at[span], dst_ref=near.at[span],
            send_sem=near_send.at[piece, k], recv_sem=near_recv.at[piece, k],
            device_id=(me, 1 - side), device_id_type=MESH,
        )

    for piece in range(PIECES):
        for k in range(3):
            load(piece, k).start()
    fetches = [
        pltpu.make_async_copy(ahead_hbm, ahead, table_sem.at[0]),
        pltpu.make_async_copy(back_hbm, back, table_sem.at[1]),
    ]

    def local(piece):
        for k in range(2):
            load(piece, k).wait()
        places = [piece * PIECE + row for row in range(PIECE)]
        for row, term in enumerate(own_term([[(ref[e, 0], ref[e, 1]) for ref in (vg, vs)] for e in places])):
            own[row] = term

    pl.semaphore_wait(barrier, 10)

    for piece in range(PIECES):
        for k in range(2):
            exchange(piece, k).start()
    for other in lines[1]:
        pl.semaphore_signal(plane_sem, inc=1, device_id=(other, side), device_id_type=MESH)
    for copy in fetches:
        copy.start()

    count = counts(mask[...])
    for half in range(HALVES):
        rows = slice(64 * half, 64 * (half + 1))
        index[half] = columns_of(count[rows])
        rank[half] = jnp.maximum(count[rows] - 1, 0)
        keep[half] = mask[rows, :].astype(F32)

    pl.semaphore_wait(plane_sem, 3)
    for other in lines[2]:
        pl.semaphore_signal(whole_sem, inc=1, device_id=(other, side), device_id_type=MESH)
    local(0)

    mine = pl.ds(pl.multiple_of(me * 8, 8), 8)

    at_x, at_z, at_y = (
        [lax.rem(lax.rem(me // stride, 4) + step, 4) * stride for step in range(4)] for stride in (16, 4, 1)
    )

    def spread_out(source, place, send_to, recv_from):
        lead = (slice(None),) * (len(source.shape) - 2)

        for a, b, c in OFFSETS:
            target = at_x[a] + at_z[b] + at_y[c]
            pltpu.make_async_remote_copy(
                src_ref=source.at[(*lead, pl.ds(pl.multiple_of(target * 8, 8), 8))], dst_ref=place.at[(*lead, mine)],
                send_sem=send_to, recv_sem=recv_from, device_id=(target, side), device_id_type=MESH,
            ).start()
        pltpu.make_async_copy(source.at[(*lead, mine)], place.at[(*lead, mine)], recv_from).start()

    def send_first(piece):
        spread_out(send.at[0, piece], recv.at[0, piece], send_sem.at[0, piece], recv_sem.at[0, piece])

    early, final = pl.ds(0, PIECES - 1), pl.ds(PIECES - 1, 1)

    def send_second(group, k):
        spread_out(send.at[1, group], recv.at[1, group], send_sem.at[1, k], recv_sem.at[1, k])

    def arrived(place, sem):
        pltpu.make_async_copy(place, place, sem).wait()

    def one_piece(piece, carry):
        load(piece, 2).wait()
        for k in range(2):
            exchange(piece, k).wait_recv()
        places = [piece * PIECE + row for row in range(PIECE)]
        terms = coupled_terms([[(ref[e, 0], ref[e, 1]) for ref in (vu, vv, vt)] for e in places])
        for row, (e, term) in enumerate(zip(places, terms)):
            term = term + own[row]
            lr, li = term[:, :128], term[:, 128:]
            gr, gi = lr + (vg[e, 0] - jnp.transpose(vg[e, 0])), li + (vg[e, 1] + jnp.transpose(vg[e, 1]))
            for half in range(HALVES):
                rows = slice(64 * half, 64 * (half + 1))
                for part, (lesser, greater) in enumerate(((lr, gr), (li, gi))):
                    send[half, piece, pl.ds(row * 2 + part, devices, stride=8), :] = packed(
                        lesser[rows], greater[rows], index[half]
                    )

        @pl.when(piece == 0)
        def _():
            pl.semaphore_wait(whole_sem, 3)

        send_first(piece)

        @pl.when(piece + 1 < PIECES)
        def _():
            local(piece + 1)

        return carry

    lax.fori_loop(0, PIECES, one_piece, 0)
    for copy in fetches:
        copy.wait()

    send_second(early, 0)
    send_second(final, 1)

    spectrum[...] = jnp.zeros(spectrum.shape, F32)

    def take_first(piece, carry):
        arrived(recv.at[0, piece], recv_sem.at[0, piece])
        forward(0, piece, recv, ahead, spread, spectrum)
        return carry

    lax.fori_loop(0, PIECES - 1, take_first, 0)
    arrived(recv.at[0, PIECES - 1], recv_sem.at[0, PIECES - 1])
    turn_back(0, PIECES - 1, recv, ahead, back, spread, spectrum, folded)
    for chunk in range(CHUNKS):
        pack_back(0, chunk, folded, psend)
        spread_out(psend.at[0, chunk], precv.at[0, chunk], back_send.at[0, chunk], back_recv.at[0, chunk])
    spectrum[...] = jnp.zeros(spectrum.shape, F32)
    arrived(recv.at[1, early], recv_sem.at[1, 0])

    def take_second(piece, carry):
        forward(1, piece, recv, ahead, spread, spectrum)
        return carry

    lax.fori_loop(0, PIECES - 1, take_second, 0)
    arrived(recv.at[1, final], recv_sem.at[1, 1])
    turn_back(1, PIECES - 1, recv, ahead, back, spread, spectrum, folded)

    def return_chunk(chunk, carry):
        pack_back(1, chunk, folded, psend)
        spread_out(psend.at[1, chunk], precv.at[1, chunk], back_send.at[1, chunk], back_recv.at[1, chunk])
        return carry

    lax.fori_loop(0, CHUNKS, return_chunk, 0)

    matrix = cut(coulomb[...])
    turned_matrix = cut(jnp.transpose(coulomb[...]))
    twice = each(lambda m: above(beside(m, jnp.zeros_like(m)), beside(jnp.zeros_like(m), m)), turned_matrix)

    def narrow(half, chunk):
        blocks = [
            unpacked(precv[half, chunk, pl.ds(row, devices, stride=8), :], rank[half], keep[half])
            for row in range(ROWS)
        ]
        result = product(cut(above(*blocks)), twice)
        for row in range(ROWS):
            half_done[chunk * ROWS + row, 64 * half : 64 * (half + 1), :] = result[64 * row : 64 * (row + 1)]

    def first_half(chunk, carry):
        arrived(precv.at[0, chunk], back_recv.at[0, chunk])
        narrow(0, chunk)
        return carry

    lax.fori_loop(0, CHUNKS, first_half, 0)

    def finish(chunk, carry):
        arrived(precv.at[1, chunk], back_recv.at[1, chunk])
        narrow(1, chunk)
        high, low = cut(beside(*[half_done[chunk * ROWS + row] for row in range(ROWS)]))
        full = jnp.dot(beside(*matrix), above(high, high), preferred_element_type=F32)
        full = full + jnp.dot(matrix[0], low, preferred_element_type=F32)
        for row in range(ROWS):
            out[chunk * ROWS + row, 0] = full[:, 256 * row : 256 * row + 128]
            out[chunk * ROWS + row, 1] = full[:, 256 * row + 128 : 256 * row + 256]
        return carry

    lax.fori_loop(0, CHUNKS, finish, 0)

    for piece in range(PIECES):
        for k in range(2):
            exchange(piece, k).wait_send()
    others = pl.ds(0, (devices - 1) * 8)
    for piece in range(PIECES):
        arrived(send.at[0, piece, others], send_sem.at[0, piece])
    arrived(send.at[1, early, others], send_sem.at[1, 0])
    arrived(send.at[1, final, others], send_sem.at[1, 1])
    for chunk in range(CHUNKS):
        arrived(psend.at[0, chunk, others], back_send.at[0, chunk])
        arrived(psend.at[1, chunk, others], back_send.at[1, chunk])


def on_device(devices, gr_diag, gr_upper, sigma_lesser, retained, coulomb):
    shape = gr_diag.shape
    blocks = [array.reshape(16, 2, 128, 128) for array in (gr_diag, gr_upper, sigma_lesser)]
    block = pltpu.VMEM((16, 2, 128, 128), F32)
    dma = pltpu.SemaphoreType.DMA
    anywhere = pl.BlockSpec(memory_space=pl.ANY)
    near = pl.BlockSpec(memory_space=pltpu.VMEM)
    out = pl.pallas_call(
        functools.partial(kernel, devices),
        out_shape=pltpu.VMEM((16, 2, 128, 128), F32),
        in_specs=[anywhere, anywhere, anywhere, near, near, anywhere, anywhere],
        out_specs=near,
        scratch_shapes=[
            block, block, block, block, block,
            pltpu.VMEM((PIECES, RADIX, 128, 192), BF16),
            pltpu.VMEM((2, RADIX, 128, 256), BF16),
            pltpu.VMEM((HALVES, PIECES, devices * 2 * PIECE, 128), F32),
            pltpu.VMEM((HALVES, PIECES, devices * 2 * PIECE, 128), F32),
            pltpu.VMEM((RADIX, 64, 128), F32),
            pltpu.VMEM((RADIX, 128, 256), F32),
            pltpu.VMEM((RADIX, 128, 128), F32),
            pltpu.VMEM((HALVES, CHUNKS, devices * ROWS, 128), F32),
            pltpu.VMEM((HALVES, CHUNKS, devices * ROWS, 128), F32),
            pltpu.VMEM((16, 128, 256), F32),
            pltpu.VMEM((HALVES, 64, 128), jnp.int32),
            pltpu.VMEM((HALVES, 64, 128), jnp.int32),
            pltpu.VMEM((HALVES, 64, 128), F32),
            pltpu.VMEM((PIECE, 128, 256), F32),
            dma((PIECES, 3)), dma((2,)), dma((PIECES, 2)), dma((PIECES, 2)),
            dma((HALVES, PIECES)), dma((HALVES, PIECES)), dma((HALVES, CHUNKS)), dma((HALVES, CHUNKS)),
            pltpu.SemaphoreType.REGULAR, pltpu.SemaphoreType.REGULAR,
        ],
        compiler_params=pltpu.CompilerParams(
            collective_id=0, has_side_effects=True, vmem_limit_bytes=60 * 1024 * 1024
        ),
        cost_estimate=pl.CostEstimate(flops=10**10, bytes_accessed=2 * 10**7, transcendentals=0),
    )(
        *blocks, retained.reshape(128, 128), coulomb.reshape(128, 128),
        jnp.asarray(ahead_tables()), jnp.asarray(back_tables()),
    )
    return out.reshape(shape)


def solution(mesh):
    whole = P("energy", None, "space", None, None)
    part = P("space", None, None)
    return jax.shard_map(
        functools.partial(on_device, mesh.shape["energy"]),
        mesh=mesh,
        in_specs=(whole, whole, whole, part, part),
        out_specs=whole,
        check_vma=False,
    )
```
